256 devices in a mesh: expert: 16 (over x_hi, y, core), blk: 16 (over x_lo, z).
Axes of the slice: x: 4 (x_hi: 2, x_lo: 2; x = x_hi * 2 + x_lo), y: 4, z: 8, core: 2. Of those that a mesh axis runs over, the one named last changes fastest.
Arguments:
- tokens: bfloat16 [2048, 6144], P(('expert', 'blk')), may hold values from -6 to 6
- out_grad: bfloat16 [2048, 6144], P(('expert', 'blk')), may hold values from -6 to 6
- expert_ids: int32 [2048, 4], P(('expert', 'blk')), may hold values from 0 to 15, as said below
- slots: int32 [2048, 4], P(('expert', 'blk')), may hold values from 0 to 2, as said below
- gates: bfloat16 [2048, 4], P(('expert', 'blk')), may hold values from 0.099609375 to 0.59765625
- w_in: bfloat16 [16, 5376, 6144], P('expert', 'blk'), may hold values from -0.078125 to 0.078125
- w_down: bfloat16 [16, 5376, 6144], P('expert', 'blk'), may hold values from -0.078125 to 0.078125
Outputs:
- grad_tokens: bfloat16 [2048, 6144], P(('expert', 'blk'))
- grad_gates: bfloat16 [2048, 4], P(('expert', 'blk'))
The draws below stay inside these ranges and needn't reach their ends.
Inputs may be any that keep to these rules, and one draw needn't show every extreme that they name: `expert_ids`: within the 8 tokens of one device, a token names 4 different experts, no expert is named more than 3 times, and one expert is named exactly 3 times by every device. Among the entries of one device that name one expert, the slots are 0 to their count minus 1, each once.
All inputs are finite; a program needn't handle non-finite values.
Results may differ from the reference program's by a relative error of at most 0.019.
Values may be sent and summed in bfloat16 or wider, within the bound.
A program may use at most 128 MiB of HBM per device.

```python
import jax
import jax.numpy as jnp
from jax import lax

D = 6144
FF = 5376
TOP = 4
TOK_DEV = 8
EXPERTS = 16
CAP = 3
TOKENS = 2048
N_BLK = 16


def routing_table(key):
    blocks = TOKENS // TOK_DEV
    key_full, key_blocks = jax.random.split(jax.random.fold_in(key, 7))
    full_expert = jax.random.randint(key_full, (), 0, EXPERTS).astype(jnp.int32)

    def one_block(block_key):
        key_order, key_tokens = jax.random.split(block_key)
        others = jax.random.permutation(key_order, EXPERTS - 1).astype(jnp.int32) + 1
        ordering = jnp.concatenate([jnp.zeros((1,), jnp.int32), others])
        position = jnp.arange(TOK_DEV * TOP, dtype=jnp.int32)
        rank_of = position // CAP
        slot_of = position % CAP
        label = (full_expert + ordering[rank_of]) % EXPERTS
        label = label.reshape(TOP, TOK_DEV).T
        slot_of = slot_of.reshape(TOP, TOK_DEV).T
        shuffle = jax.random.permutation(key_tokens, TOK_DEV)
        return (label[shuffle], slot_of[shuffle])
    labels, places = jax.vmap(one_block)(jax.random.split(key_blocks, blocks))
    return (labels.reshape(TOKENS, TOP).astype(jnp.int32), places.reshape(TOKENS, TOP).astype(jnp.int32))


def draw_expert_ids(key, part):
    return routing_table(key)[0]


def draw_slots(key, part):
    return routing_table(key)[1]


def block_levels(own_key, dims, shards, least, top_value):
    def one(axis_at, parts):
        heights = jax.random.uniform(jax.random.fold_in(jax.random.fold_in(own_key, 6), axis_at), (parts,), jnp.float32, least / len(shards), top_value / len(shards))
        return jnp.repeat(jnp.exp(heights), dims[axis_at] // parts).reshape((-1,) + (1,) * (len(dims) - axis_at - 1))

    gain = one(*shards[0])
    for cut in shards[1:]:
        gain = gain * one(*cut)
    return gain


def normal_values(rng, shape, width, bound, cuts=(), held_as=jnp.bfloat16):
    array = width * jax.random.normal(rng, shape, jnp.float32)
    if cuts:
        array = array * block_levels(rng, shape, cuts, -0.22, 0.18)
    return jnp.clip(array, -bound, bound).astype(held_as)


def setup_inputs(seed: int = 0) -> dict:
    key_of = jax.random.split(jax.random.key(seed), 8)
    tokens = normal_values(key_of[0], (TOKENS, D), 1.0, 6.0, ((0, 256),))
    out_grad = normal_values(key_of[1], (TOKENS, D), 1.0, 6.0, ((0, 256),))
    expert_ids = draw_expert_ids(jax.random.fold_in(key_of[7], 71), 0)
    slots = draw_slots(jax.random.fold_in(key_of[7], 71), 0)
    gates = jnp.clip(0.099609375 + 0.49804688 * jax.random.uniform(key_of[4], (TOKENS, TOP), jnp.float32) ** block_levels(key_of[4], (TOKENS, TOP), ((0, 256),), -0.2, 0.2), 0.099609375, 0.59765625).astype(jnp.bfloat16)
    w_in = normal_values(key_of[5], (EXPERTS, FF, D), D ** -0.5, 0.078125, ((0, 16), (1, 16)))
    w_down = normal_values(key_of[6], (EXPERTS, FF, D), D ** -0.5, 0.078125, ((0, 16), (1, 16)))
    return dict(tokens=tokens, out_grad=out_grad, expert_ids=expert_ids, slots=slots, gates=gates, w_in=w_in, w_down=w_down)


def block_tables(ids_block, slots_block, gates_block):
    target = (ids_block * CAP + slots_block).reshape(-1)
    owner = jnp.broadcast_to(jnp.arange(TOK_DEV, dtype=jnp.int32)[:, None], (TOK_DEV, TOP)).reshape(-1)
    table = jnp.full((EXPERTS * CAP,), TOK_DEV, dtype=jnp.int32).at[target].set(owner)
    weight = jnp.zeros((EXPERTS * CAP,), jnp.bfloat16).at[target].set(gates_block.reshape(-1))
    return table, weight


def reference(tokens, out_grad, expert_ids, slots, gates, w_in, w_down):
    blocks = TOKENS // TOK_DEV
    tables, weights = jax.vmap(block_tables)(expert_ids.reshape(blocks, TOK_DEV, TOP), slots.reshape(blocks, TOK_DEV, TOP), gates.reshape(blocks, TOK_DEV, TOP))
    base = (jnp.arange(blocks, dtype=jnp.int32) * TOK_DEV)[:, None]
    row_index = jnp.where(tables == TOK_DEV, TOKENS, base + tables).astype(jnp.int32)
    x_padded = jnp.concatenate([tokens, jnp.zeros((1, D), jnp.bfloat16)], axis=0)
    dy_padded = jnp.concatenate([out_grad, jnp.zeros((1, D), jnp.bfloat16)], axis=0)
    group = FF // N_BLK

    def per_expert(expert):
        picks = lax.dynamic_slice_in_dim(row_index, expert * CAP, CAP, 1).reshape(-1)
        scales = lax.dynamic_slice_in_dim(weights, expert * CAP, CAP, 1).reshape(-1)
        rows_x = x_padded[picks]
        rows_dy = dy_padded[picks]
        weight_in = w_in[expert]
        weight_down = w_down[expert]
        pre = jnp.dot(rows_x, weight_in.T, preferred_element_type=jnp.float32)
        back = jnp.dot(rows_dy, weight_down.T, preferred_element_type=jnp.float32)
        sigma = jax.nn.sigmoid(pre)
        gate_grad = jnp.sum(pre * sigma * back, axis=1).astype(jnp.bfloat16)
        slope = (scales.astype(jnp.float32)[:, None] * back * sigma * (1.0 + pre * (1.0 - sigma))).astype(jnp.bfloat16)
        pieces = jnp.einsum("rbf,bfd->rbd", slope.reshape(-1, N_BLK, group).astype(jnp.float32), weight_in.reshape(N_BLK, group, D).astype(jnp.float32))
        rounded = lax.optimization_barrier(pieces.astype(jnp.bfloat16)).astype(jnp.float32)
        row_grad = jnp.sum(rounded, axis=1).astype(jnp.bfloat16)
        return row_grad, gate_grad

    row_grads, gate_grads = lax.map(per_expert, jnp.arange(EXPERTS, dtype=jnp.int32))
    token_block = (jnp.arange(TOKENS, dtype=jnp.int32) // TOK_DEV)[:, None]
    where = (token_block * CAP + slots).astype(jnp.int32)
    picked = row_grads[expert_ids, where].astype(jnp.float32)
    grad_tokens = jnp.sum(picked, axis=1).astype(jnp.bfloat16)
    grad_gates = gate_grads[expert_ids, where]
    return grad_tokens, grad_gates
```

```python
import functools

import jax
import jax.numpy as jnp
from jax import lax
from jax.experimental import pallas as pl
from jax.experimental.pallas import tpu as pltpu
from jax.sharding import PartitionSpec as P

MESH = pl.DeviceIdType.MESH
RING = 8
LANES = 128


def nt(a, b):
    return lax.dot_general(a, b, (((1,), (1,)), ((), ())), preferred_element_type=jnp.float32)


def kernel(
    rows_ref, win_ref, wdn_ref, out_ref,
    X, WI, WD, PRE, BACK, ES, ER, SL, PART, SU, SD, RU, RD,
    loc_sem, ws_sem, wr_sem, us_sem, ur_sem, ds_sem, dr_sem, es_sem, er_sem,
    rus_sem, rur_sem, rds_sem, rdr_sem,
):
    R, half = rows_ref.shape[0], rows_ref.shape[1] // 2
    U = R // 2
    blk = lax.axis_index("blk")
    xl, z = blk // RING, blk % RING
    above = {"blk": xl * RING + (z + 1) % RING}
    below = {"blk": xl * RING + (z + RING - 1) % RING}
    pair = {"blk": (1 - xl) * RING + z}

    barrier = pltpu.get_barrier_semaphore()
    for peer in (above, below, pair):
        pl.semaphore_signal(barrier, inc=1, device_id=peer, device_id_type=MESH)

    mine = pl.ds(pl.multiple_of(xl * half, LANES), half)
    theirs = pl.ds(pl.multiple_of((1 - xl) * half, LANES), half)
    local = [
        pltpu.make_async_copy(rows_ref, X.at[0, pl.ds(R, R), :], loc_sem.at[0]),
        pltpu.make_async_copy(win_ref.at[:, mine], WI.at[xl], loc_sem.at[1]),
        pltpu.make_async_copy(wdn_ref.at[:, mine], WD.at[xl], loc_sem.at[2]),
    ]
    for c in local:
        c.start()

    def remote(src, dst, ss, rs, peer):
        return pltpu.make_async_remote_copy(
            src_ref=src, dst_ref=dst, send_sem=ss, recv_sem=rs, device_id=peer, device_id_type=MESH
        )

    pl.semaphore_wait(barrier, 3)

    weights_out = [
        remote(win_ref.at[:, theirs], WI.at[xl], ws_sem.at[0], wr_sem.at[0], pair),
        remote(wdn_ref.at[:, theirs], WD.at[xl], ws_sem.at[1], wr_sem.at[1], pair),
    ]
    for c in weights_out:
        c.start()

    def up(s, u):
        src = X.at[0, pl.ds(R + u * U, U), :] if s == 1 else X.at[s - 1, pl.ds(u * U, U), :]
        dst = X.at[s % 4, pl.ds(u * U, U), :]
        return remote(src, dst, us_sem.at[s - 1, u], ur_sem.at[s - 1, u], above)

    def down(s, u):
        src = X.at[(s - 1) % 4, pl.ds(R + u * U, U), :]
        dst = X.at[s, pl.ds(R + u * U, U), :] if s < 4 else X.at[0, pl.ds(u * U, U), :]
        return remote(src, dst, ds_sem.at[s - 1, u], dr_sem.at[s - 1, u], below)

    local[0].wait()
    for u in range(2):
        up(1, u).start()
        down(1, u).start()
    local[1].wait()
    local[2].wait()

    def project(q, h):
        PRE[q, h] = nt(X[q, :, :half], WI[h])
        BACK[q, h] = nt(X[q, :, half:], WD[h])

    for s in range(1, 4):
        for u in range(2):
            up(s, u).wait_recv()
            if s < 3 or u == 0:
                up(s + 1, u).start()
            down(s, u).wait_recv()
            if s < 3 or u == 1:
                down(s + 1, u).start()
        project(s, xl)
    up(4, 0).wait_recv()
    down(4, 1).wait_recv()
    project(0, xl)
    remote(win_ref.at[:, mine], WI.at[1 - xl], ws_sem.at[0], wr_sem.at[0], pair).wait_recv()
    remote(wdn_ref.at[:, mine], WD.at[1 - xl], ws_sem.at[1], wr_sem.at[1], pair).wait_recv()

    def swap(k):
        q, at, n = ((0, 0, R), (3, 0, 2 * R), (2, 0, 2 * R), (1, 0, 2 * R), (0, R, R))[k]
        there = (q, slice(None), slice(None), pl.ds(at, n), slice(None))
        return remote(ES.at[there], ER.at[there], es_sem.at[k], er_sem.at[k], pair)

    def project_and_send(k):
        q = (0, 3, 2, 1)[k]
        project(q, 1 - xl)
        for h in range(2):
            ES[q, 0, h] = PRE[q, h].astype(jnp.bfloat16)
            ES[q, 1, h] = BACK[q, h].astype(jnp.bfloat16)
        swap(k).start()
        if k == 3:
            swap(4).start()

    def terms(k):
        q, at, n = ((0, 0, R), (3, 0, 2 * R), (2, 0, 2 * R), (1, 0, 2 * R), (0, R, R))[k]
        rows = pl.ds(at, n)
        swap(k).wait_recv()
        gate = jnp.zeros((n, 1), jnp.float32)
        for h in range(2):
            pre = PRE[q, h, rows, :] + ER[q, 0, h, rows, :].astype(jnp.float32)
            back = BACK[q, h, rows, :] + ER[q, 1, h, rows, :].astype(jnp.float32)
            sigma = jax.nn.sigmoid(pre)
            act = pre * sigma
            gate = gate + jnp.sum(act * back, axis=1, keepdims=True)
            SL[h, rows, :] = (back * sigma * (1.0 + pre * (1.0 - sigma))).astype(jnp.bfloat16)
        PART[rows, pl.ds(half, LANES)] = jnp.broadcast_to(gate, (n, LANES))
        step = 4 * LANES

        def columns(c, carry):
            there = pl.ds(pl.multiple_of(c * step, step), step)
            PART[rows, there] = jnp.dot(
                SL[0, rows, :], WI[0, :, there], preferred_element_type=jnp.float32
            ) + jnp.dot(SL[1, rows, :], WI[1, :, there], preferred_element_type=jnp.float32)
            return carry

        lax.fori_loop(0, half // step, columns, 0)

    def sum_up(i, u):
        rows = pl.ds(u * U, U)
        return remote(SU.at[i, rows, :], RU.at[i, rows, :], rus_sem.at[i, u], rur_sem.at[i, u], above)

    def sum_down(i, u):
        rows = pl.ds(u * U, U)
        return remote(SD.at[i, rows, :], RD.at[i, rows, :], rds_sem.at[i, u], rdr_sem.at[i, u], below)

    project_and_send(0)
    project_and_send(1)
    terms(0)
    SU[0, 0:U, :] = PART[0:U, :].astype(jnp.bfloat16)
    sum_up(0, 0).start()
    SD[0, U:R, :] = PART[U:R, :].astype(jnp.bfloat16)
    sum_down(0, 1).start()
    for k in range(1, 4):
        if k < 3:
            project_and_send(k + 1)
        terms(k)
        for u in range(2):
            own = slice(u * U, u * U + U)
            term = PART[R + u * U : R + u * U + U, :]
            if k > 1 or u == 0:
                sum_up(k - 1, u).wait_recv()
                term = term + RU[k - 1, own, :].astype(jnp.float32)
            SU[k, own, :] = term.astype(jnp.bfloat16)
            sum_up(k, u).start()
            term = PART[own, :]
            if k > 1 or u == 1:
                sum_down(k - 1, u).wait_recv()
                term = term + RD[k - 1, own, :].astype(jnp.float32)
            SD[k, own, :] = term.astype(jnp.bfloat16)
            sum_down(k, u).start()
    terms(4)
    for u in range(2):
        own = slice(u * U, u * U + U)
        sum_up(3, u).wait_recv()
        sum_down(3, u).wait_recv()
        out_ref[own, :] = (
            PART[R + u * U : R + u * U + U, :]
            + RU[3, own, :].astype(jnp.float32)
            + RD[3, own, :].astype(jnp.float32)
        ).astype(out_ref.dtype)

    for c in weights_out:
        c.wait_send()
    for s in range(1, 5):
        for u in range(2):
            if s < 4 or u == 0:
                up(s, u).wait_send()
            if s < 4 or u == 1:
                down(s, u).wait_send()
    for k in range(5):
        swap(k).wait_send()
    for i in range(4):
        for u in range(2):
            if i > 0 or u == 0:
                sum_up(i, u).wait_send()
            if i > 0 or u == 1:
                sum_down(i, u).wait_send()


def expert_rows(rows, w_in, w_down):
    n_rows, width = rows.shape
    half, hidden = width // 2, w_in.shape[0]
    wide = half + LANES
    bf16, f32, dma = jnp.bfloat16, jnp.float32, pltpu.SemaphoreType.DMA
    return pl.pallas_call(
        kernel,
        out_shape=jax.ShapeDtypeStruct((n_rows, wide), bf16),
        in_specs=[pl.BlockSpec(memory_space=pl.ANY)] * 3,
        out_specs=pl.BlockSpec(memory_space=pltpu.VMEM),
        scratch_shapes=[
            pltpu.VMEM((4, 2 * n_rows, width), bf16),
            pltpu.VMEM((2, hidden, half), bf16),
            pltpu.VMEM((2, hidden, half), bf16),
            pltpu.VMEM((4, 2, 2 * n_rows, hidden), f32),
            pltpu.VMEM((4, 2, 2 * n_rows, hidden), f32),
            pltpu.VMEM((4, 2, 2, 2 * n_rows, hidden), bf16),
            pltpu.VMEM((4, 2, 2, 2 * n_rows, hidden), bf16),
            pltpu.VMEM((2, 2 * n_rows, hidden), bf16),
            pltpu.VMEM((2 * n_rows, wide), f32),
            pltpu.VMEM((4, n_rows, wide), bf16),
            pltpu.VMEM((4, n_rows, wide), bf16),
            pltpu.VMEM((4, n_rows, wide), bf16),
            pltpu.VMEM((4, n_rows, wide), bf16),
            dma((3,)), dma((2,)), dma((2,)),
            dma((4, 2)), dma((4, 2)), dma((4, 2)), dma((4, 2)),
            dma((5,)), dma((5,)),
            dma((4, 2)), dma((4, 2)), dma((4, 2)), dma((4, 2)),
        ],
        compiler_params=pltpu.CompilerParams(
            collective_id=0, has_side_effects=True, vmem_limit_bytes=60 * 2**20
        ),
    )(rows, w_in, w_down)


def per_device(tokens, out_grad, expert_ids, slots, gates, w_in, w_down):
    tok_count, width = tokens.shape
    half = width // 2
    top_count = expert_ids.shape[1]
    expert_count, blk_count = lax.axis_size("expert"), lax.axis_size("blk")
    capacity = max(2, (tok_count * top_count + expert_count - 1) // expert_count + 1)
    swap = [(i, (i + RING) % blk_count) for i in range(blk_count)]
    xl = lax.axis_index("blk") // RING

    def cut(a, side):
        return lax.dynamic_slice(a, (0, side * half), (tok_count, half))

    small = jnp.concatenate(
        [(expert_ids * (2 * capacity) + slots + capacity * xl).astype(jnp.bfloat16), gates], axis=1
    )
    small = jnp.pad(small, ((0, 0), (0, LANES - 2 * top_count)))
    away = jnp.concatenate([cut(tokens, 1 - xl), cut(out_grad, 1 - xl), small], axis=1)
    stay = jnp.concatenate([cut(tokens, xl), cut(out_grad, xl), small], axis=1)
    came = lax.ppermute(away, "blk", swap)
    both = jnp.concatenate([stay, came], axis=0)
    target = both[:, width : width + top_count].astype(jnp.int32)
    weight = both[:, width + top_count : width + 2 * top_count].astype(jnp.float32)
    slot_count = expert_count * 2 * capacity
    matches = (target[None] == jnp.arange(slot_count, dtype=jnp.int32)[:, None, None]).astype(
        jnp.float32
    )
    placing = jnp.sum(matches, axis=2).astype(jnp.bfloat16)
    weighed = jnp.sum(matches * weight[None], axis=2).astype(jnp.bfloat16)
    send = jnp.dot(placing, both[:, :width], preferred_element_type=jnp.float32).astype(jnp.bfloat16)
    rows = lax.all_to_all(send, "expert", split_axis=0, concat_axis=0, tiled=True)
    grads = expert_rows(rows, w_in[0], w_down[0])
    back = lax.all_to_all(grads, "expert", split_axis=0, concat_axis=0, tiled=True)
    grad = lax.dot_general(
        weighed, back[:, :half], (((0,), (0,)), ((), ())), preferred_element_type=jnp.float32
    ).astype(jnp.bfloat16)
    own, other = grad[:tok_count], grad[tok_count:]
    other = lax.ppermute(other, "blk", swap)
    grad_tokens = jnp.where(
        xl == 0, jnp.concatenate([own, other], axis=1), jnp.concatenate([other, own], axis=1)
    )
    grad_gates = jnp.einsum(
        "stk,s->tk", matches[:, :tok_count], back[:, half].astype(jnp.float32)
    ).astype(jnp.bfloat16)
    return (grad_tokens, grad_gates)


def solution(mesh):
    return jax.shard_map(
        per_device,
        mesh=mesh,
        in_specs=(
            P(("expert", "blk"), None),
            P(("expert", "blk"), None),
            P(("expert", "blk"), None),
            P(("expert", "blk"), None),
            P(("expert", "blk"), None),
            P("expert", "blk", None),
            P("expert", "blk", None),
        ),
        out_specs=(P(("expert", "blk"), None), P(("expert", "blk"), None)),
        check_vma=False,
    )
```

```python
import functools

import jax
import jax.numpy as jnp
from jax import lax
from jax.experimental import pallas as pl
from jax.experimental.pallas import tpu as pltpu
from jax.sharding import PartitionSpec as P

MESH = pl.DeviceIdType.MESH
RING = 8
LANES = 128


def nt(a, b):
    return lax.dot_general(a, b, (((1,), (1,)), ((), ())), preferred_element_type=jnp.float32)


GROUPS = ((3, 0), (0, 0), (2, 0), (3, 1), (1, 0), (2, 1), (1, 1), (0, 1))
BEFORE = (None, None, (0, False), (1, True), (2, False), (3, False), (5, False))
CHUNKS = 8


def kernel(
    send_ref, win_ref, wdn_ref, out_ref,
    GOT, X, WI, WD, PRE, BACK, ES, ER, SL, PART, SUM, ARR, MIX, TURN, TS,
    loc_sem, ws_sem, wr_sem, us_sem, ur_sem, ds_sem, dr_sem, es_sem, er_sem,
    ss_sem, sr_sem, as_sem, ar_sem, bs_sem, br_sem,
):
    half, hidden = WI.shape[2], WI.shape[1]
    R = X.shape[1] // 2
    U = R // 2
    bf16, f32 = jnp.bfloat16, jnp.float32
    n_exp = lax.axis_size("expert")
    me = lax.axis_index("expert")
    blk = lax.axis_index("blk")
    xl, z = blk // RING, blk % RING
    above = {"blk": xl * RING + (z + 1) % RING}
    below = {"blk": xl * RING + (z + RING - 1) % RING}
    pair = {"blk": (1 - xl) * RING + z}

    def remote(src, dst, ss, rs, peer):
        return pltpu.make_async_remote_copy(
            src_ref=src, dst_ref=dst, send_sem=ss, recv_sem=rs, device_id=peer, device_id_type=MESH
        )

    def expert_loop(body):
        lax.fori_loop(1, n_exp, lambda j, c: (body(j), c)[1], 0)

    def greet(j):
        peer = {"expert": (me + j) % n_exp}
        pl.semaphore_signal(barrier, inc=1, device_id=peer, device_id_type=MESH)

    barrier = pltpu.get_barrier_semaphore()
    expert_loop(greet)
    for peer in (above, below, pair):
        pl.semaphore_signal(barrier, inc=1, device_id=peer, device_id_type=MESH)

    T = send_ref.shape[0] // n_exp

    def piece(e):
        return pl.ds(pl.multiple_of(e * T, 16), T)

    mine = pl.ds(pl.multiple_of(xl * half, LANES), half)
    theirs = pl.ds(pl.multiple_of((1 - xl) * half, LANES), half)
    own_rows = pltpu.make_async_copy(send_ref.at[piece(me), :], GOT.at[piece(me), :], loc_sem.at[0])
    own_win = pltpu.make_async_copy(win_ref.at[:, mine], WI.at[xl], loc_sem.at[1])
    own_wdn = pltpu.make_async_copy(wdn_ref.at[:, mine], WD.at[xl], loc_sem.at[2])

    out_win = remote(win_ref.at[:, theirs], WI.at[xl], ws_sem.at[0], wr_sem.at[0], pair)
    out_wdn = remote(wdn_ref.at[:, theirs], WD.at[xl], ws_sem.at[1], wr_sem.at[1], pair)
    in_win = remote(win_ref.at[:, mine], WI.at[1 - xl], ws_sem.at[0], wr_sem.at[0], pair)
    in_wdn = remote(wdn_ref.at[:, mine], WD.at[1 - xl], ws_sem.at[1], wr_sem.at[1], pair)

    def to_expert(j):
        e = (me + j) % n_exp
        return remote(
            send_ref.at[piece(e), :], GOT.at[piece(me), :], as_sem.at[j], ar_sem.at[j], {"expert": e}
        )

    def to_token(j):
        e = (me + j) % n_exp
        return remote(TS.at[piece(e), :], out_ref.at[piece(me), :], bs_sem.at[j], br_sem.at[j], {"expert": e})

    own_rows.start()
    pl.semaphore_wait(barrier, n_exp - 1 + 3)
    expert_loop(lambda j: to_expert(j).start())
    out_win.start()
    own_win.start()
    own_wdn.start()

    size = CHUNKS * U
    slots = T // CHUNKS
    row = lax.broadcasted_iota(jnp.int32, (size, 1), 0)
    partner = ((row // slots) % CHUNKS) * U + (row // U) * slots + row % slots
    MIX[...] = (lax.broadcasted_iota(jnp.int32, (size, size), 1) == partner).astype(f32).astype(bf16)

    def at_below(u):
        return pl.ds(2 * U * u, U)

    def at_above(u):
        return pl.ds(U if u == 1 else 3 * U, U)

    def up(s, u):
        src = X.at[0, pl.ds(R + u * U, U), :] if s == 1 else X.at[s - 1, at_below(u), :]
        dst = X.at[s, at_below(u), :] if s < 4 else X.at[0, pl.ds(u * U, U), :]
        return remote(src, dst, us_sem.at[s - 1, u], ur_sem.at[s - 1, u], above)

    def down(s, u):
        src = X.at[0, pl.ds(R + u * U, U), :] if s == 1 else X.at[s - 1, at_above(u), :]
        dst = X.at[s, at_above(u), :] if s < 4 else X.at[0, pl.ds(u * U, U), :]
        return remote(src, dst, ds_sem.at[s - 1, u], dr_sem.at[s - 1, u], below)

    own_rows.wait()
    expert_loop(lambda j: to_expert(j).wait_recv())
    wide = GOT.shape[1]
    for u in range(2):
        TURN[...] = jnp.dot(
            MIX[...], GOT[u * size : u * size + size, :], preferred_element_type=f32
        ).astype(bf16)
        for k in range(CHUNKS):
            X[0, R + u * U : R + u * U + U, k * wide : (k + 1) * wide] = TURN[k * U : (k + 1) * U, :]
        if u == 0:
            up(1, 0).start()
    down(1, 1).start()
    up(1, 1).start()
    down(1, 0).start()
    own_win.wait()
    own_wdn.wait()

    def project(q, at, n, h, what):
        rows = pl.ds(at, n)
        if "p" in what:
            PRE[q, h, rows, :] = nt(X[q, rows, :half], WI[h])
        if "b" in what:
            BACK[q, h, rows, :] = nt(X[q, rows, half:], WD[h])

    project(0, R, R, xl, "pb")
    for s in range(1, 4):
        up(s, 0).wait_recv()
        up(s + 1, 0).start()
        down(s, 1).wait_recv()
        down(s + 1, 1).start()
        if s == 3:
            project(3, 0, R, xl, "pb")
        up(s, 1).wait_recv()
        if s < 3:
            up(s + 1, 1).start()
        down(s, 0).wait_recv()
        if s < 3:
            down(s + 1, 0).start()
            if s == 1:
                out_wdn.start()
            project(s, 0, 2 * R, xl, "pb")
        else:
            project(3, R, R, xl, "pb")
        if s == 2:
            in_win.wait_recv()
            project(1, 0, 2 * R, 1 - xl, "p")
            project(2, 0, 2 * R, 1 - xl, "p")
    project(3, 0, 2 * R, 1 - xl, "p")

    def swap(k):
        return remote(ES.at[k], ER.at[k], es_sem.at[k], er_sem.at[k], pair)

    def give(k):
        q, at = GROUPS[k][0], GROUPS[k][1] * R
        for h in range(2):
            ES[k, 0, h] = PRE[q, h, at : at + R, :].astype(bf16)
            ES[k, 1, h] = BACK[q, h, at : at + R, :].astype(bf16)
        swap(k).start()

    def terms(k):
        q, at = GROUPS[k][0], GROUPS[k][1] * R
        swap(k).wait_recv()
        gate = jnp.zeros((R, 1), f32)
        for h in range(2):
            pre = PRE[q, h, at : at + R, :] + ER[k, 0, h].astype(f32)
            back = BACK[q, h, at : at + R, :] + ER[k, 1, h].astype(f32)
            sigma = jax.nn.sigmoid(pre)
            act = pre * sigma
            gate = gate + jnp.sum(act * back, axis=1, keepdims=True)
            SL[h] = (back * sigma * (1.0 + pre * (1.0 - sigma))).astype(bf16)
        PART[:, half:] = jnp.broadcast_to(gate, (R, LANES))
        step = 4 * LANES

        def columns(c, carry):
            there = pl.ds(pl.multiple_of(c * step, step), step)
            PART[:, there] = jnp.dot(SL[0], WI[0, :, there], preferred_element_type=f32) + jnp.dot(
                SL[1], WI[1, :, there], preferred_element_type=f32
            )
            return carry

        lax.fori_loop(0, half // step, columns, 0)

    def pass_on(k, a):
        rows = pl.ds(a * U, U)
        peer = above if (a == 0) == (k == 1) else below
        return remote(SUM.at[k, rows, :], ARR.at[k, rows, :], ss_sem.at[k, a], sr_sem.at[k, a], peer)

    def arrived(k, a):
        pass_on(k, a).wait_recv()
        return ARR[k, a * U : a * U + U, :].astype(f32)

    def add_and_pass(k):
        terms(k)
        for a in range(2):
            term = PART[a * U : a * U + U, :]
            if BEFORE[k] is not None:
                b, crossed = BEFORE[k]
                term = term + arrived(b, 1 - a if crossed else a)
            SUM[k, a * U : a * U + U, :] = term.astype(bf16)
            pass_on(k, a).start()

    in_wdn.wait_recv()
    project(3, 0, 2 * R, 1 - xl, "b")
    give(0)
    project(2, 0, 2 * R, 1 - xl, "b")
    up(4, 0).wait_recv()
    down(4, 1).wait_recv()
    project(0, 0, R, xl, "pb")
    project(0, 0, 2 * R, 1 - xl, "pb")
    give(1)
    give(2)
    project(1, 0, 2 * R, 1 - xl, "b")
    add_and_pass(0)
    give(3)
    for k in range(1, 7):
        add_and_pass(k)
        if k + 3 < 8:
            give(k + 3)
    terms(7)

    def send_out(j):
        to_token(j).start()

    for a in range(2):
        total = (PART[a * U : a * U + U, :] + arrived(4, a) + arrived(6, 1 - a)).astype(bf16)
        third = half // CHUNKS
        for k in range(CHUNKS):
            TURN[k * U : (k + 1) * U, :third] = total[:, k * third : (k + 1) * third]
            TURN[k * U : (k + 1) * U, third : third + LANES] = total[:, half:]
        TS[a * size : a * size + size, :] = jnp.dot(
            MIX[...], TURN[:, : third + LANES], preferred_element_type=f32
        ).astype(bf16)
    expert_loop(send_out)
    own_back = pltpu.make_async_copy(TS.at[piece(me), :], out_ref.at[piece(me), :], loc_sem.at[3])
    own_back.start()

    out_win.wait_send()
    out_wdn.wait_send()
    expert_loop(lambda j: to_expert(j).wait_send())
    for s in range(1, 5):
        for u in range(2):
            if s < 4 or u == 0:
                up(s, u).wait_send()
            if s < 4 or u == 1:
                down(s, u).wait_send()
    for k in range(8):
        swap(k).wait_send()
    for k in range(7):
        for a in range(2):
            pass_on(k, a).wait_send()
    own_back.wait()
    expert_loop(lambda j: to_token(j).wait())


def expert_rows(send, w_in, w_down, slots):
    n_exp = lax.axis_size("expert")
    hidden, width = w_in.shape
    half = width // 2
    n_rows = n_exp * slots
    wide = half + LANES
    back = half // CHUNKS + LANES
    bf16, f32, dma = jnp.bfloat16, jnp.float32, pltpu.SemaphoreType.DMA
    return pl.pallas_call(
        kernel,
        out_shape=jax.ShapeDtypeStruct((send.shape[0], back), bf16),
        in_specs=[pl.BlockSpec(memory_space=pl.ANY)] * 3,
        out_specs=pl.BlockSpec(memory_space=pltpu.VMEM),
        scratch_shapes=[
            pltpu.VMEM(send.shape, bf16),
            pltpu.VMEM((4, 2 * n_rows, width), bf16),
            pltpu.VMEM((2, hidden, half), bf16),
            pltpu.VMEM((2, hidden, half), bf16),
            pltpu.VMEM((4, 2, 2 * n_rows, hidden), f32),
            pltpu.VMEM((4, 2, 2 * n_rows, hidden), f32),
            pltpu.VMEM((8, 2, 2, n_rows, hidden), bf16),
            pltpu.VMEM((8, 2, 2, n_rows, hidden), bf16),
            pltpu.VMEM((2, n_rows, hidden), bf16),
            pltpu.VMEM((n_rows, wide), f32),
            pltpu.VMEM((7, n_rows, wide), bf16),
            pltpu.VMEM((7, n_rows, wide), bf16),
            pltpu.VMEM((send.shape[0] // 2, send.shape[0] // 2), bf16),
            pltpu.VMEM((send.shape[0] // 2, send.shape[1]), bf16),
            pltpu.VMEM((send.shape[0], back), bf16),
            dma((4,)), dma((2,)), dma((2,)),
            dma((4, 2)), dma((4, 2)), dma((4, 2)), dma((4, 2)),
            dma((8,)), dma((8,)),
            dma((7, 2)), dma((7, 2)),
            dma((n_exp,)), dma((n_exp,)), dma((n_exp,)), dma((n_exp,)),
        ],
        compiler_params=pltpu.CompilerParams(
            collective_id=0, has_side_effects=True, vmem_limit_bytes=60 * 2**20
        ),
    )(send, w_in, w_down)


def per_device(tokens, out_grad, expert_ids, slots, gates, w_in, w_down):
    tok_count, width = tokens.shape
    half = width // 2
    top_count = expert_ids.shape[1]
    expert_count, blk_count = lax.axis_size("expert"), lax.axis_size("blk")
    capacity = max(2, (tok_count * top_count + expert_count - 1) // expert_count + 1)
    swap = [(i, (i + RING) % blk_count) for i in range(blk_count)]
    xl = lax.axis_index("blk") // RING

    def cut(a, side):
        return lax.dynamic_slice(a, (0, side * half), (tok_count, half))

    small = jnp.concatenate(
        [(expert_ids * (2 * capacity) + slots + capacity * xl).astype(jnp.bfloat16), gates], axis=1
    )
    small = jnp.pad(small, ((0, 0), (0, LANES - 2 * top_count)))
    away = jnp.concatenate([cut(tokens, 1 - xl), cut(out_grad, 1 - xl), small], axis=1)
    stay = jnp.concatenate([cut(tokens, xl), cut(out_grad, xl), small], axis=1)
    came = lax.ppermute(away, "blk", swap)
    both = jnp.concatenate([stay, came], axis=0)
    target = both[:, width : width + top_count].astype(jnp.int32)
    weight = both[:, width + top_count : width + 2 * top_count].astype(jnp.float32)
    slot_count = 2 * capacity
    n_tok = 2 * tok_count
    row = jnp.arange(expert_count * CHUNKS * slot_count, dtype=jnp.int32)
    row_target = row // (CHUNKS * slot_count) * slot_count + row % slot_count
    row_piece = row // slot_count % CHUNKS
    matches = (target[None] == row_target[:, None, None]).astype(jnp.float32)
    placing = jnp.sum(matches, axis=2)
    weighed = jnp.sum(matches * weight[None], axis=2)
    same = (row_piece[:, None] == jnp.arange(CHUNKS)[None]).astype(jnp.float32)

    def pieces(a):
        return (same[:, :, None] * a[:, None, :]).reshape(row.shape[0], CHUNKS * n_tok).astype(jnp.bfloat16)

    piece = width // CHUNKS
    stacked = jnp.concatenate([both[:, k * piece : (k + 1) * piece] for k in range(CHUNKS)], axis=0)
    send = jnp.dot(pieces(placing), stacked, preferred_element_type=jnp.float32).astype(jnp.bfloat16)
    back = expert_rows(send, w_in[0], w_down[0], slot_count)
    part = half // CHUNKS
    grad = lax.dot_general(
        pieces(weighed), back[:, :part], (((0,), (0,)), ((), ())), preferred_element_type=jnp.float32
    ).astype(jnp.bfloat16)
    grad = jnp.concatenate([grad[k * n_tok : (k + 1) * n_tok] for k in range(CHUNKS)], axis=1)
    own, other = grad[:tok_count], grad[tok_count:]
    other = lax.ppermute(other, "blk", swap)
    grad_tokens = jnp.where(
        xl == 0, jnp.concatenate([own, other], axis=1), jnp.concatenate([other, own], axis=1)
    )
    first = (row_piece == 0).astype(jnp.float32) * back[:, part].astype(jnp.float32)
    grad_gates = jnp.einsum("stk,s->tk", matches[:, :tok_count], first).astype(jnp.bfloat16)
    return (grad_tokens, grad_gates)


def solution(mesh):
    return jax.shard_map(
        per_device,
        mesh=mesh,
        in_specs=(
            P(("expert", "blk"), None),
            P(("expert", "blk"), None),
            P(("expert", "blk"), None),
            P(("expert", "blk"), None),
            P(("expert", "blk"), None),
            P("expert", "blk", None),
            P("expert", "blk", None),
        ),
        out_specs=(P(("expert", "blk"), None), P(("expert", "blk"), None)),
        check_vma=False,
    )
```

```python
import functools

import jax
import jax.numpy as jnp
from jax import lax
from jax.experimental import pallas as pl
from jax.experimental.pallas import tpu as pltpu
from jax.sharding import PartitionSpec as P

MESH = pl.DeviceIdType.MESH
RING = 8
LANES = 128


def nt(a, b):
    return lax.dot_general(a, b, (((1,), (1,)), ((), ())), preferred_element_type=jnp.float32)


GROUPS = ((3, 0), (0, 0), (2, 0), (3, 1), (1, 0), (2, 1), (1, 1), (0, 1))
BEFORE = (None, None, (0, False), (1, True), (2, False), (3, False), (5, False))
CHUNKS = 8


def kernel(
    raw_ref, far_ref, win_ref, wdn_ref, out_ref,
    RAW, OUT, GOT, FAR, X, WI, WD, PRE, BACK, ES, ER, SL, PART, SUM, ARR, MIX, TURN, TS,
    loc_sem, ws_sem, wr_sem, us_sem, ur_sem, ds_sem, dr_sem, es_sem, er_sem,
    ss_sem, sr_sem, as_sem, ar_sem, bs_sem, br_sem, ts_sem, tr_sem, ys_sem, yr_sem,
):
    half, hidden = WI.shape[2], WI.shape[1]
    R = X.shape[1] // 2
    U = R // 2
    bf16, f32 = jnp.bfloat16, jnp.float32
    n_exp = lax.axis_size("expert")
    me = lax.axis_index("expert")
    near = n_exp // 2
    side, seat = me // near, me % near
    blk = lax.axis_index("blk")
    xl, z = blk // RING, blk % RING
    above = {"blk": xl * RING + (z + 1) % RING}
    below = {"blk": xl * RING + (z + RING - 1) % RING}
    pair = {"blk": (1 - xl) * RING + z}

    def remote(src, dst, ss, rs, peer):
        return pltpu.make_async_remote_copy(
            src_ref=src, dst_ref=dst, send_sem=ss, recv_sem=rs, device_id=peer, device_id_type=MESH
        )

    def expert_loop(body):
        lax.fori_loop(1, n_exp, lambda j, c: (body(j), c)[1], 0)

    def greet(j):
        peer = {"expert": (me + j) % n_exp}
        pl.semaphore_signal(barrier, inc=1, device_id=peer, device_id_type=MESH)

    barrier = pltpu.get_barrier_semaphore()
    expert_loop(greet)
    for peer in (above, below, pair):
        pl.semaphore_signal(barrier, inc=1, device_id=peer, device_id_type=MESH)

    def across(j):
        return {"expert": (1 - side) * near + (seat + j) % near, "blk": (1 - xl) * RING + z}

    def greet_across(j, carry):
        pl.semaphore_signal(barrier, inc=1, device_id=across(j), device_id_type=MESH)
        return carry

    lax.fori_loop(0, near, greet_across, 0)

    T = far_ref.shape[0] // near

    def piece(e):
        return pl.ds(pl.multiple_of(e * T, 16), T)

    mine = pl.ds(pl.multiple_of(xl * half, LANES), half)
    theirs = pl.ds(pl.multiple_of((1 - xl) * half, LANES), half)
    own_raw = pltpu.make_async_copy(raw_ref, RAW.at[0], loc_sem.at[0])
    own_win = pltpu.make_async_copy(win_ref.at[:, mine], WI.at[xl], loc_sem.at[1])
    own_wdn = pltpu.make_async_copy(wdn_ref.at[:, mine], WD.at[xl], loc_sem.at[2])

    out_win = remote(win_ref.at[:, theirs], WI.at[xl], ws_sem.at[0], wr_sem.at[0], pair)
    out_wdn = remote(wdn_ref.at[:, theirs], WD.at[xl], ws_sem.at[1], wr_sem.at[1], pair)
    in_win = remote(win_ref.at[:, mine], WI.at[1 - xl], ws_sem.at[0], wr_sem.at[0], pair)
    in_wdn = remote(wdn_ref.at[:, mine], WD.at[1 - xl], ws_sem.at[1], wr_sem.at[1], pair)

    def to_far(j):
        e = (seat + j) % near
        return remote(far_ref.at[piece(e), :], FAR.at[piece(seat), :], as_sem.at[j], ar_sem.at[j], across(j))

    def to_near(r, j):
        e = (seat + j) % near
        return remote(
            OUT.at[r, piece(e), :], GOT.at[r, piece(seat), :], ys_sem.at[r, j], yr_sem.at[r, j],
            {"expert": side * near + e},
        )

    def near_own(r):
        return pltpu.make_async_copy(OUT.at[r, piece(seat), :], GOT.at[r, piece(seat), :], ys_sem.at[r, 0])

    def near_loop(r, body):
        lax.fori_loop(1, near, lambda j, c: (body(to_near(r, j)), c)[1], 0)

    def far_loop(body):
        lax.fori_loop(0, near, lambda j, c: (body(to_far(j)), c)[1], 0)

    def to_token(j):
        e = (me + j) % n_exp
        a = (e // near + side) % 2
        return remote(
            TS.at[piece(a * near + e % near), :], out_ref.at[piece(me), :], bs_sem.at[j], br_sem.at[j],
            {"expert": e},
        )

    def raw_rows(a):
        return pl.ds(0, 80) if a == 0 else pl.ds(80, RAW.shape[1] - 80)

    def raw_up(s, a):
        return remote(
            RAW.at[s - 1, raw_rows(a), :], RAW.at[s, raw_rows(a), :], ts_sem.at[0, s - 1, a],
            tr_sem.at[0, s - 1, a], above,
        )

    def raw_down(s, a):
        src = 0 if s == 1 else RING // 2 + s - 1
        dst = RING // 2 + s if s < 4 else 4
        return remote(
            RAW.at[src, raw_rows(a), :], RAW.at[dst, raw_rows(a), :], ts_sem.at[1, s - 1, a],
            tr_sem.at[1, s - 1, a], below,
        )

    own_raw.start()
    own_raw.wait()
    pl.semaphore_wait(barrier, n_exp - 1 + 3 + near)
    raw_up(1, 0).start()
    raw_down(1, 1).start()
    raw_up(1, 1).start()
    raw_down(1, 0).start()
    far_loop(lambda c: c.start())
    out_win.start()
    own_win.start()
    own_wdn.start()

    size = CHUNKS * U
    slots = T // CHUNKS
    row = lax.broadcasted_iota(jnp.int32, (size, 1), 0)
    partner = ((row // slots) % CHUNKS) * U + (row // U) * slots + row % slots
    MIX[...] = (lax.broadcasted_iota(jnp.int32, (size, size), 1) == partner).astype(f32).astype(bf16)

    tok = (RAW.shape[1] - 16) // CHUNKS
    wanted = ((side * near + row // T) * slots + row % slots).astype(f32)
    piece_of = (row // slots) % CHUNKS
    lane = lax.broadcasted_iota(jnp.int32, (1, CHUNKS * tok), 1) // tok

    def place(r):
        table = RAW[r, CHUNKS * tok : CHUNKS * tok + 16, : CHUNKS * tok].astype(f32)
        hit = jnp.zeros((size, CHUNKS * tok), f32)
        for k in range(4):
            hit = hit + (table[k : k + 1, :] == wanted).astype(f32)
        hit = jnp.where(piece_of == lane, hit, 0.0).astype(bf16)
        OUT[r] = jnp.dot(hit, RAW[r, : CHUNKS * tok, :], preferred_element_type=f32).astype(bf16)
        near_loop(r, lambda c: c.start())
        near_own(r).start()

    wide = FAR.shape[1]

    def turned(got, q, at):
        TURN[...] = jnp.dot(MIX[...], got, preferred_element_type=f32).astype(bf16)
        for k in range(CHUNKS):
            X[q, at : at + U, k * wide : (k + 1) * wide] = TURN[k * U : (k + 1) * U, :]

    def settle(r, q, at):
        near_own(r).wait()
        near_loop(r, lambda c: c.wait_recv())
        turned(GOT[r], q, at)

    def cols(a):
        return pl.ds(a * half, half)

    def up(s, a):
        src = X.at[0, pl.ds(3 * U, U), cols(a)] if s == 1 else X.at[s - 1, pl.ds(2 * U, U), cols(a)]
        dst = X.at[s, pl.ds(2 * U, U), cols(a)] if s < 4 else X.at[0, pl.ds(U, U), cols(a)]
        return remote(src, dst, us_sem.at[s - 1, a], ur_sem.at[s - 1, a], above)

    def down(s, a):
        src = X.at[0, pl.ds(3 * U, U), cols(a)] if s == 1 else X.at[s - 1, pl.ds(U, U), cols(a)]
        dst = X.at[s % 4, pl.ds(U, U), cols(a)]
        return remote(src, dst, ds_sem.at[s - 1, a], dr_sem.at[s - 1, a], below)

    place(0)
    for s in range(1, 4):
        raw_up(s, 0).wait_recv()
        raw_up(s + 1, 0).start()
        raw_down(s, 1).wait_recv()
        raw_down(s + 1, 1).start()
        raw_up(s, 1).wait_recv()
        if s < 3:
            raw_up(s + 1, 1).start()
        raw_down(s, 0).wait_recv()
        if s < 3:
            raw_down(s + 1, 0).start()
        else:
            far_loop(lambda c: c.wait_recv())
            turned(FAR[...], 0, 3 * U)
            up(1, 0).start()
            down(1, 1).start()
            up(1, 1).start()
            down(1, 0).start()
        place(s)
        place(RING // 2 + s)
    raw_up(4, 0).wait_recv()
    raw_down(4, 1).wait_recv()
    place(4)
    own_win.wait()
    own_wdn.wait()
    settle(0, 0, 2 * U)

    def project(q, at, n, h, what):
        rows = pl.ds(at, n)
        if "p" in what:
            PRE[q, h, rows, :] = nt(X[q, rows, :half], WI[h])
        if "b" in what:
            BACK[q, h, rows, :] = nt(X[q, rows, half:], WD[h])

    project(0, R, R, xl, "pb")
    for s in range(1, 4):
        up(s, 0).wait_recv()
        up(s + 1, 0).start()
        down(s, 1).wait_recv()
        down(s + 1, 1).start()
        up(s, 1).wait_recv()
        if s < 3:
            up(s + 1, 1).start()
        down(s, 0).wait_recv()
        if s < 3:
            down(s + 1, 0).start()
        if s == 1:
            out_wdn.start()
        settle(s, s, 0)
        settle(RING // 2 + s, s, 3 * U)
        project(s, 0, 2 * R, xl, "pb")
    up(4, 0).wait_recv()
    down(4, 1).wait_recv()
    settle(4, 0, 0)
    project(0, 0, R, xl, "pb")
    in_win.wait_recv()
    for q in range(4):
        project(q, 0, 2 * R, 1 - xl, "p")

    def swap(k):
        return remote(ES.at[k], ER.at[k], es_sem.at[k], er_sem.at[k], pair)

    def give(k):
        q, at = GROUPS[k][0], GROUPS[k][1] * R
        for h in range(2):
            ES[k, 0, h] = PRE[q, h, at : at + R, :].astype(bf16)
            ES[k, 1, h] = BACK[q, h, at : at + R, :].astype(bf16)
        swap(k).start()

    def terms(k):
        q, at = GROUPS[k][0], GROUPS[k][1] * R
        swap(k).wait_recv()
        gate = jnp.zeros((R, 1), f32)
        for h in range(2):
            pre = PRE[q, h, at : at + R, :] + ER[k, 0, h].astype(f32)
            back = BACK[q, h, at : at + R, :] + ER[k, 1, h].astype(f32)
            sigma = jax.nn.sigmoid(pre)
            act = pre * sigma
            gate = gate + jnp.sum(act * back, axis=1, keepdims=True)
            SL[h] = (back * sigma * (1.0 + pre * (1.0 - sigma))).astype(bf16)
        PART[:, half:] = jnp.broadcast_to(gate, (R, LANES))
        step = 4 * LANES

        def columns(c, carry):
            there = pl.ds(pl.multiple_of(c * step, step), step)
            PART[:, there] = jnp.dot(SL[0], WI[0, :, there], preferred_element_type=f32) + jnp.dot(
                SL[1], WI[1, :, there], preferred_element_type=f32
            )
            return carry

        lax.fori_loop(0, half // step, columns, 0)

    def pass_on(k, a):
        rows = pl.ds(a * U, U)
        peer = above if (a == 0) == (k == 1) else below
        return remote(SUM.at[k, rows, :], ARR.at[k, rows, :], ss_sem.at[k, a], sr_sem.at[k, a], peer)

    def arrived(k, a):
        pass_on(k, a).wait_recv()
        return ARR[k, a * U : a * U + U, :].astype(f32)

    def add_and_pass(k):
        terms(k)
        for a in range(2):
            term = PART[a * U : a * U + U, :]
            if BEFORE[k] is not None:
                b, crossed = BEFORE[k]
                term = term + arrived(b, 1 - a if crossed else a)
            SUM[k, a * U : a * U + U, :] = term.astype(bf16)
            pass_on(k, a).start()

    in_wdn.wait_recv()
    project(3, 0, 2 * R, 1 - xl, "b")
    give(0)
    project(0, 0, 2 * R, 1 - xl, "b")
    give(1)
    project(2, 0, 2 * R, 1 - xl, "b")
    give(2)
    project(1, 0, 2 * R, 1 - xl, "b")
    add_and_pass(0)
    give(3)
    for k in range(1, 7):
        add_and_pass(k)
        if k + 3 < 8:
            give(k + 3)
    terms(7)

    def send_out(j):
        to_token(j).start()

    for a in range(2):
        total = (PART[a * U : a * U + U, :] + arrived(4, a) + arrived(6, 1 - a)).astype(bf16)
        third = half // CHUNKS
        for k in range(CHUNKS):
            TURN[k * U : (k + 1) * U, :third] = total[:, k * third : (k + 1) * third]
            TURN[k * U : (k + 1) * U, third : third + LANES] = total[:, half:]
        TS[a * size : a * size + size, :] = jnp.dot(
            MIX[...], TURN[:, : third + LANES], preferred_element_type=f32
        ).astype(bf16)
    expert_loop(send_out)
    own_back = pltpu.make_async_copy(TS.at[piece(seat), :], out_ref.at[piece(me), :], loc_sem.at[3])
    own_back.start()

    out_win.wait_send()
    out_wdn.wait_send()
    far_loop(lambda c: c.wait_send())
    for r in range(RING):
        near_loop(r, lambda c: c.wait_send())
    for s in range(1, 5):
        for a in range(2):
            if s < 4 or a == 0:
                raw_up(s, a).wait_send()
            if s < 4 or a == 1:
                raw_down(s, a).wait_send()
    for s in range(1, 5):
        for u in range(2):
            if s < 4 or u == 0:
                up(s, u).wait_send()
            if s < 4 or u == 1:
                down(s, u).wait_send()
    for k in range(8):
        swap(k).wait_send()
    for k in range(7):
        for a in range(2):
            pass_on(k, a).wait_send()
    own_back.wait()
    expert_loop(lambda j: to_token(j).wait())


def expert_rows(raw, far, w_in, w_down, slots):
    n_exp = lax.axis_size("expert")
    hidden, width = w_in.shape
    half = width // 2
    n_rows = n_exp * slots
    wide = half + LANES
    back = half // CHUNKS + LANES
    bf16, f32, dma = jnp.bfloat16, jnp.float32, pltpu.SemaphoreType.DMA
    return pl.pallas_call(
        kernel,
        out_shape=jax.ShapeDtypeStruct((2 * far.shape[0], back), bf16),
        in_specs=[pl.BlockSpec(memory_space=pl.ANY)] * 4,
        out_specs=pl.BlockSpec(memory_space=pltpu.VMEM),
        scratch_shapes=[
            pltpu.VMEM((RING,) + raw.shape, bf16),
            pltpu.VMEM((RING,) + far.shape, bf16),
            pltpu.VMEM((RING,) + far.shape, bf16),
            pltpu.VMEM(far.shape, bf16),
            pltpu.VMEM((4, 2 * n_rows, width), bf16),
            pltpu.VMEM((2, hidden, half), bf16),
            pltpu.VMEM((2, hidden, half), bf16),
            pltpu.VMEM((4, 2, 2 * n_rows, hidden), f32),
            pltpu.VMEM((4, 2, 2 * n_rows, hidden), f32),
            pltpu.VMEM((8, 2, 2, n_rows, hidden), bf16),
            pltpu.VMEM((8, 2, 2, n_rows, hidden), bf16),
            pltpu.VMEM((2, n_rows, hidden), bf16),
            pltpu.VMEM((n_rows, wide), f32),
            pltpu.VMEM((7, n_rows, wide), bf16),
            pltpu.VMEM((7, n_rows, wide), bf16),
            pltpu.VMEM((far.shape[0], far.shape[0]), bf16),
            pltpu.VMEM(far.shape, bf16),
            pltpu.VMEM((2 * far.shape[0], back), bf16),
            dma((4,)), dma((2,)), dma((2,)),
            dma((4, 2)), dma((4, 2)), dma((4, 2)), dma((4, 2)),
            dma((8,)), dma((8,)),
            dma((7, 2)), dma((7, 2)),
            dma((n_exp // 2,)), dma((n_exp // 2,)), dma((n_exp,)), dma((n_exp,)),
            dma((2, 4, 2)), dma((2, 4, 2)), dma((RING, n_exp // 2)), dma((RING, n_exp // 2)),
        ],
        compiler_params=pltpu.CompilerParams(
            collective_id=0, has_side_effects=True, vmem_limit_bytes=60 * 2**20
        ),
    )(raw, far, w_in, w_down)


def per_device(tokens, out_grad, expert_ids, slots, gates, w_in, w_down):
    tok_count, width = tokens.shape
    half = width // 2
    top_count = expert_ids.shape[1]
    expert_count, blk_count = lax.axis_size("expert"), lax.axis_size("blk")
    capacity = max(2, (tok_count * top_count + expert_count - 1) // expert_count + 1)
    swap = [(i, (i + RING) % blk_count) for i in range(blk_count)]
    xl = lax.axis_index("blk") // RING

    def cut(a, at, side):
        return lax.dynamic_slice(a, (0, at * width + side * half), (tok_count, half))

    small = jnp.concatenate(
        [(expert_ids * (2 * capacity) + slots + capacity * xl).astype(jnp.bfloat16), gates], axis=1
    )
    small = jnp.pad(small, ((0, 0), (0, LANES - 2 * top_count)))
    away = jnp.concatenate([tokens, out_grad, small], axis=1)
    came = lax.ppermute(away, "blk", swap)
    small = jnp.concatenate([small, came[:, 2 * width :]], axis=0)
    target = small[:, :top_count].astype(jnp.int32)
    weight = small[:, top_count : 2 * top_count].astype(jnp.float32)
    slot_count = 2 * capacity
    n_tok = 2 * tok_count
    row = jnp.arange(expert_count * CHUNKS * slot_count, dtype=jnp.int32)
    row_target = row // (CHUNKS * slot_count) * slot_count + row % slot_count
    row_piece = row // slot_count % CHUNKS
    matches = (target[None] == row_target[:, None, None]).astype(jnp.float32)
    placing = jnp.sum(matches, axis=2)
    weighed = jnp.sum(matches * weight[None], axis=2)
    same = (row_piece[:, None] == jnp.arange(CHUNKS)[None]).astype(jnp.float32)

    def pieces(a):
        return (same[:, :, None] * a[:, None, :]).reshape(row.shape[0], CHUNKS * n_tok).astype(jnp.bfloat16)

    def stacked(side):
        rows = [
            jnp.concatenate([cut(a, 0, side), cut(b, at, side)], axis=1)
            for a, b, at in ((tokens, out_grad, 0), (came, came, 1))
        ]
        both = jnp.concatenate(rows, axis=0)
        piece = width // CHUNKS
        return jnp.concatenate([both[:, k * piece : (k + 1) * piece] for k in range(CHUNKS)], axis=0)

    near = row.shape[0] // 2
    x_hi = lax.axis_index("expert") // (expert_count // 2)
    raw = stacked(xl)
    table = jnp.tile(small[:, :top_count].T, (1, CHUNKS))
    table = jnp.pad(table, ((0, 16 - top_count), (0, raw.shape[1] - table.shape[1])), constant_values=-1)
    raw = jnp.concatenate([raw, table], axis=0)
    far = lax.dynamic_slice(pieces(placing), ((1 - x_hi) * near, 0), (near, CHUNKS * n_tok))
    far = jnp.dot(far, stacked(1 - xl), preferred_element_type=jnp.float32).astype(jnp.bfloat16)
    back = expert_rows(raw, far, w_in[0], w_down[0], slot_count)
    part = half // CHUNKS
    grad = lax.dot_general(
        pieces(weighed), back[:, :part], (((0,), (0,)), ((), ())), preferred_element_type=jnp.float32
    ).astype(jnp.bfloat16)
    grad = jnp.concatenate([grad[k * n_tok : (k + 1) * n_tok] for k in range(CHUNKS)], axis=1)
    own, other = grad[:tok_count], grad[tok_count:]
    other = lax.ppermute(other, "blk", swap)
    grad_tokens = jnp.where(
        xl == 0, jnp.concatenate([own, other], axis=1), jnp.concatenate([other, own], axis=1)
    )
    first = (row_piece == 0).astype(jnp.float32) * back[:, part].astype(jnp.float32)
    grad_gates = jnp.einsum("stk,s->tk", matches[:, :tok_count], first).astype(jnp.bfloat16)
    return (grad_tokens, grad_gates)


def solution(mesh):
    return jax.shard_map(
        per_device,
        mesh=mesh,
        in_specs=(
            P(("expert", "blk"), None),
            P(("expert", "blk"), None),
            P(("expert", "blk"), None),
            P(("expert", "blk"), None),
            P(("expert", "blk"), None),
            P("expert", "blk", None),
            P("expert", "blk", None),
        ),
        out_specs=(P(("expert", "blk"), None), P(("expert", "blk"), None)),
        check_vma=False,
    )
```

```python
import functools

import jax
import jax.numpy as jnp
from jax import lax
from jax.experimental import pallas as pl
from jax.experimental.pallas import tpu as pltpu
from jax.sharding import PartitionSpec as P

MESH = pl.DeviceIdType.MESH
RING = 8
LANES = 128


def nt(a, b):
    return lax.dot_general(a, b, (((1,), (1,)), ((), ())), preferred_element_type=jnp.float32)


GROUPS = ((3, 0), (0, 0), (2, 0), (3, 1), (1, 0), (2, 1), (1, 1), (0, 1))
BEFORE = (None, None, (0, False), (1, True), (2, False), (3, False), (5, False))
CHUNKS = 8
THIRD = 3


def kernel(
    raw_ref, far_ref, win_ref, wdn_ref, out_ref,
    RAW, OUT, GOT, FAR, X, WI, WD, WP, PRE, BACK, ES, ER, SL, PART, SUM, ARR, MIX, TURN, TS,
    loc_sem, ws_sem, wr_sem, us_sem, ur_sem, ds_sem, dr_sem, es_sem, er_sem,
    ss_sem, sr_sem, as_sem, ar_sem, bs_sem, br_sem, ts_sem, tr_sem, ys_sem, yr_sem,
):
    half, hidden = WI.shape[2], WI.shape[1]
    R = X.shape[1] // 2
    U = R // 2
    bf16, f32 = jnp.bfloat16, jnp.float32
    n_exp = lax.axis_size("expert")
    me = lax.axis_index("expert")
    near = n_exp // 2
    side, seat = me // near, me % near
    blk = lax.axis_index("blk")
    xl, z = blk // RING, blk % RING
    above = {"blk": xl * RING + (z + 1) % RING}
    below = {"blk": xl * RING + (z + RING - 1) % RING}
    pair = {"blk": (1 - xl) * RING + z}

    def remote(src, dst, ss, rs, peer):
        return pltpu.make_async_remote_copy(
            src_ref=src, dst_ref=dst, send_sem=ss, recv_sem=rs, device_id=peer, device_id_type=MESH
        )

    def expert_loop(body):
        lax.fori_loop(1, n_exp, lambda j, c: (body(j), c)[1], 0)

    def greet(j):
        peer = {"expert": (me + j) % n_exp}
        pl.semaphore_signal(barrier, inc=1, device_id=peer, device_id_type=MESH)

    barrier = pltpu.get_barrier_semaphore()
    expert_loop(greet)
    for peer in (above, below, pair):
        pl.semaphore_signal(barrier, inc=1, device_id=peer, device_id_type=MESH)

    def across(j):
        return {"expert": (1 - side) * near + (seat + j) % near, "blk": (1 - xl) * RING + z}

    def greet_across(j, carry):
        pl.semaphore_signal(barrier, inc=1, device_id=across(j), device_id_type=MESH)
        return carry

    lax.fori_loop(0, near, greet_across, 0)

    T = far_ref.shape[0] // near

    def piece(e):
        return pl.ds(pl.multiple_of(e * T, 16), T)

    mine = pl.ds(pl.multiple_of(xl * half, LANES), half)
    theirs = pl.ds(pl.multiple_of((1 - xl) * half, LANES), half)
    own_raw = pltpu.make_async_copy(raw_ref, RAW.at[0], loc_sem.at[0])
    own_win = pltpu.make_async_copy(win_ref.at[:, mine], WI.at[xl], loc_sem.at[1])
    share = WP.shape[1]
    my_part = pl.ds(pl.multiple_of(xl * share, LANES), share)
    their_part = pl.ds(pl.multiple_of((1 - xl) * share, LANES), share)
    rest = pl.ds(2 * share, share)
    own_wdn = [
        pltpu.make_async_copy(wdn_ref.at[:, my_part], WD.at[:, pl.ds(0, share)], loc_sem.at[2]),
        pltpu.make_async_copy(wdn_ref.at[:, rest], WD.at[:, pl.ds(share, share)], loc_sem.at[4]),
    ]

    out_win = remote(win_ref.at[:, theirs], WI.at[xl], ws_sem.at[0], wr_sem.at[0], pair)
    out_wdn = remote(wdn_ref.at[:, their_part], WP, ws_sem.at[1], wr_sem.at[1], pair)
    in_win = remote(win_ref.at[:, mine], WI.at[1 - xl], ws_sem.at[0], wr_sem.at[0], pair)

    def to_far(j):
        e = (seat + j) % near
        return remote(far_ref.at[piece(e), :], FAR.at[piece(seat), :], as_sem.at[j], ar_sem.at[j], across(j))

    def to_near(r, j):
        e = (seat + j) % near
        return remote(
            OUT.at[r, piece(e), :], GOT.at[r, piece(seat), :], ys_sem.at[r, j], yr_sem.at[r, j],
            {"expert": side * near + e},
        )

    def near_own(r):
        return pltpu.make_async_copy(OUT.at[r, piece(seat), :], GOT.at[r, piece(seat), :], ys_sem.at[r, 0])

    def near_loop(r, body):
        lax.fori_loop(1, near, lambda j, c: (body(to_near(r, j)), c)[1], 0)

    def far_loop(body):
        lax.fori_loop(0, near, lambda j, c: (body(to_far(j)), c)[1], 0)

    def to_token(j):
        e = (me + j) % n_exp
        a = (e // near + side) % 2
        return remote(
            TS.at[piece(a * near + e % near), :], out_ref.at[piece(me), :], bs_sem.at[j], br_sem.at[j],
            {"expert": e},
        )

    def raw_rows(a):
        return pl.ds(0, 80) if a == 0 else pl.ds(80, RAW.shape[1] - 80)

    def raw_up(s, a):
        return remote(
            RAW.at[s - 1, raw_rows(a), :], RAW.at[s, raw_rows(a), :], ts_sem.at[0, s - 1, a],
            tr_sem.at[0, s - 1, a], above,
        )

    def raw_down(s, a):
        src = 0 if s == 1 else RING // 2 + s - 1
        dst = RING // 2 + s if s < 4 else 4
        return remote(
            RAW.at[src, raw_rows(a), :], RAW.at[dst, raw_rows(a), :], ts_sem.at[1, s - 1, a],
            tr_sem.at[1, s - 1, a], below,
        )

    own_raw.start()
    own_raw.wait()
    pl.semaphore_wait(barrier, n_exp - 1 + 3 + near)
    raw_up(1, 0).start()
    raw_down(1, 1).start()
    raw_up(1, 1).start()
    raw_down(1, 0).start()
    far_loop(lambda c: c.start())
    out_win.start()
    own_win.start()
    for c in own_wdn:
        c.start()

    size = CHUNKS * U
    slots = T // CHUNKS
    row = lax.broadcasted_iota(jnp.int32, (size, 1), 0)
    partner = ((row // slots) % CHUNKS) * U + (row // U) * slots + row % slots
    MIX[...] = (lax.broadcasted_iota(jnp.int32, (size, size), 1) == partner).astype(f32).astype(bf16)

    tok = (RAW.shape[1] - 16) // CHUNKS
    wanted = ((side * near + row // T) * slots + row % slots).astype(f32)
    piece_of = (row // slots) % CHUNKS
    lane = lax.broadcasted_iota(jnp.int32, (1, CHUNKS * tok), 1) // tok

    def place(r):
        table = RAW[r, CHUNKS * tok : CHUNKS * tok + 16, : CHUNKS * tok].astype(f32)
        hit = jnp.zeros((size, CHUNKS * tok), f32)
        for k in range(4):
            hit = hit + (table[k : k + 1, :] == wanted).astype(f32)
        hit = jnp.where(piece_of == lane, hit, 0.0).astype(bf16)
        OUT[r] = jnp.dot(hit, RAW[r, : CHUNKS * tok, :], preferred_element_type=f32).astype(bf16)
        near_loop(r, lambda c: c.start())
        near_own(r).start()

    wide = FAR.shape[1]

    def turned(got, q, at):
        TURN[...] = jnp.dot(MIX[...], got, preferred_element_type=f32).astype(bf16)
        for k in range(CHUNKS):
            X[q, at : at + U, k * wide : (k + 1) * wide] = TURN[k * U : (k + 1) * U, :]

    def settle(r, q, at):
        near_own(r).wait()
        near_loop(r, lambda c: c.wait_recv())
        turned(GOT[r], q, at)

    def cols(a):
        return pl.ds(a * (X.shape[2] // 2), X.shape[2] // 2)

    def up(s, a):
        src = X.at[0, pl.ds(3 * U, U), cols(a)] if s == 1 else X.at[s - 1, pl.ds(2 * U, U), cols(a)]
        dst = X.at[s, pl.ds(2 * U, U), cols(a)] if s < 4 else X.at[0, pl.ds(U, U), cols(a)]
        return remote(src, dst, us_sem.at[s - 1, a], ur_sem.at[s - 1, a], above)

    def down(s, a):
        src = X.at[0, pl.ds(3 * U, U), cols(a)] if s == 1 else X.at[s - 1, pl.ds(U, U), cols(a)]
        dst = X.at[s % 4, pl.ds(U, U), cols(a)]
        return remote(src, dst, ds_sem.at[s - 1, a], dr_sem.at[s - 1, a], below)

    place(0)
    for s in range(1, 4):
        raw_up(s, 0).wait_recv()
        raw_up(s + 1, 0).start()
        raw_down(s, 1).wait_recv()
        raw_down(s + 1, 1).start()
        raw_up(s, 1).wait_recv()
        if s < 3:
            raw_up(s + 1, 1).start()
        raw_down(s, 0).wait_recv()
        if s < 3:
            raw_down(s + 1, 0).start()
        else:
            far_loop(lambda c: c.wait_recv())
            turned(FAR[...], 0, 3 * U)
            up(1, 0).start()
            down(1, 1).start()
            up(1, 1).start()
            down(1, 0).start()
        place(s)
        place(RING // 2 + s)
    raw_up(4, 0).wait_recv()
    raw_down(4, 1).wait_recv()
    place(4)
    own_win.wait()
    for c in own_wdn:
        c.wait()
    settle(0, 0, 2 * U)

    def project(q, at, n, h, what):
        rows = pl.ds(at, n)
        if "p" in what:
            PRE[q, h, rows, :] = nt(X[q, rows, :half], WI[h])
        if "b" in what:
            BACK[q, h, rows, :] = nt(X[q, rows, half:], WD[...])
        if "r" in what:
            BACK[q, h, rows, :] = nt(X[q, rows, half : half + share], WP[...])

    project(0, R, R, xl, "pb")
    for s in range(1, 4):
        up(s, 0).wait_recv()
        up(s + 1, 0).start()
        down(s, 1).wait_recv()
        down(s + 1, 1).start()
        up(s, 1).wait_recv()
        if s < 3:
            up(s + 1, 1).start()
        down(s, 0).wait_recv()
        if s < 3:
            down(s + 1, 0).start()
        if s == 1:
            out_wdn.start()
        settle(s, s, 0)
        settle(RING // 2 + s, s, 3 * U)
        project(s, 0, 2 * R, xl, "pb")
    up(4, 0).wait_recv()
    down(4, 1).wait_recv()
    settle(4, 0, 0)
    project(0, 0, R, xl, "pb")
    in_win.wait_recv()
    for q in range(4):
        project(q, 0, 2 * R, 1 - xl, "p")

    def swap(k):
        return remote(ES.at[k], ER.at[k], es_sem.at[k], er_sem.at[k], pair)

    def give(k):
        q, at = GROUPS[k][0], GROUPS[k][1] * R
        for h in range(2):
            ES[k, 0, h] = PRE[q, h, at : at + R, :].astype(bf16)
            ES[k, 1, h] = BACK[q, h, at : at + R, :].astype(bf16)
        swap(k).start()

    def terms(k):
        q, at = GROUPS[k][0], GROUPS[k][1] * R
        swap(k).wait_recv()
        gate = jnp.zeros((R, 1), f32)
        for h in range(2):
            pre = PRE[q, h, at : at + R, :] + ER[k, 0, h].astype(f32)
            back = BACK[q, h, at : at + R, :] + ER[k, 1, h].astype(f32)
            sigma = jax.nn.sigmoid(pre)
            act = pre * sigma
            gate = gate + jnp.sum(act * back, axis=1, keepdims=True)
            SL[h] = (back * sigma * (1.0 + pre * (1.0 - sigma))).astype(bf16)
        PART[:, half:] = jnp.broadcast_to(gate, (R, LANES))
        step = 4 * LANES

        def columns(c, carry):
            there = pl.ds(pl.multiple_of(c * step, step), step)
            PART[:, there] = jnp.dot(SL[0], WI[0, :, there], preferred_element_type=f32) + jnp.dot(
                SL[1], WI[1, :, there], preferred_element_type=f32
            )
            return carry

        lax.fori_loop(0, half // step, columns, 0)

    def pass_on(k, a):
        rows = pl.ds(a * U, U)
        peer = above if (a == 0) == (k == 1) else below
        return remote(SUM.at[k, rows, :], ARR.at[k, rows, :], ss_sem.at[k, a], sr_sem.at[k, a], peer)

    def arrived(k, a):
        pass_on(k, a).wait_recv()
        return ARR[k, a * U : a * U + U, :].astype(f32)

    def add_and_pass(k):
        terms(k)
        for a in range(2):
            term = PART[a * U : a * U + U, :]
            if BEFORE[k] is not None:
                b, crossed = BEFORE[k]
                term = term + arrived(b, 1 - a if crossed else a)
            SUM[k, a * U : a * U + U, :] = term.astype(bf16)
            pass_on(k, a).start()

    out_wdn.wait_recv()
    project(3, 0, 2 * R, 1 - xl, "r")
    give(0)
    project(0, 0, 2 * R, 1 - xl, "r")
    give(1)
    project(2, 0, 2 * R, 1 - xl, "r")
    give(2)
    project(1, 0, 2 * R, 1 - xl, "r")
    add_and_pass(0)
    give(3)
    for k in range(1, 7):
        add_and_pass(k)
        if k + 3 < 8:
            give(k + 3)
    terms(7)

    def send_out(j):
        to_token(j).start()

    for a in range(2):
        total = (PART[a * U : a * U + U, :] + arrived(4, a) + arrived(6, 1 - a)).astype(bf16)
        third = half // CHUNKS
        for k in range(CHUNKS):
            TURN[k * U : (k + 1) * U, :third] = total[:, k * third : (k + 1) * third]
            TURN[k * U : (k + 1) * U, third : third + LANES] = total[:, half:]
        TS[a * size : a * size + size, :] = jnp.dot(
            MIX[...], TURN[:, : third + LANES], preferred_element_type=f32
        ).astype(bf16)
    expert_loop(send_out)
    own_back = pltpu.make_async_copy(TS.at[piece(seat), :], out_ref.at[piece(me), :], loc_sem.at[3])
    own_back.start()

    out_win.wait_send()
    out_wdn.wait_send()
    far_loop(lambda c: c.wait_send())
    for r in range(RING):
        near_loop(r, lambda c: c.wait_send())
    for s in range(1, 5):
        for a in range(2):
            if s < 4 or a == 0:
                raw_up(s, a).wait_send()
            if s < 4 or a == 1:
                raw_down(s, a).wait_send()
    for s in range(1, 5):
        for u in range(2):
            if s < 4 or u == 0:
                up(s, u).wait_send()
            if s < 4 or u == 1:
                down(s, u).wait_send()
    for k in range(8):
        swap(k).wait_send()
    for k in range(7):
        for a in range(2):
            pass_on(k, a).wait_send()
    own_back.wait()
    expert_loop(lambda j: to_token(j).wait())


def expert_rows(raw, far, w_in, w_down, slots):
    n_exp = lax.axis_size("expert")
    hidden, width = w_in.shape
    half = width // 2
    n_rows = n_exp * slots
    wide = half + LANES
    back = half // CHUNKS + LANES
    bf16, f32, dma = jnp.bfloat16, jnp.float32, pltpu.SemaphoreType.DMA
    return pl.pallas_call(
        kernel,
        out_shape=jax.ShapeDtypeStruct((2 * far.shape[0], back), bf16),
        in_specs=[pl.BlockSpec(memory_space=pl.ANY)] * 4,
        out_specs=pl.BlockSpec(memory_space=pltpu.VMEM),
        scratch_shapes=[
            pltpu.VMEM((RING,) + raw.shape, bf16),
            pltpu.VMEM((RING,) + far.shape, bf16),
            pltpu.VMEM((RING,) + far.shape, bf16),
            pltpu.VMEM(far.shape, bf16),
            pltpu.VMEM((4, 2 * n_rows, CHUNKS * raw.shape[1]), bf16),
            pltpu.VMEM((2, hidden, half), bf16),
            pltpu.VMEM((hidden, 2 * width // THIRD), bf16),
            pltpu.VMEM((hidden, width // THIRD), bf16),
            pltpu.VMEM((4, 2, 2 * n_rows, hidden), f32),
            pltpu.VMEM((4, 2, 2 * n_rows, hidden), f32),
            pltpu.VMEM((8, 2, 2, n_rows, hidden), bf16),
            pltpu.VMEM((8, 2, 2, n_rows, hidden), bf16),
            pltpu.VMEM((2, n_rows, hidden), bf16),
            pltpu.VMEM((n_rows, wide), f32),
            pltpu.VMEM((7, n_rows, wide), bf16),
            pltpu.VMEM((7, n_rows, wide), bf16),
            pltpu.VMEM((far.shape[0], far.shape[0]), bf16),
            pltpu.VMEM(far.shape, bf16),
            pltpu.VMEM((2 * far.shape[0], back), bf16),
            dma((5,)), dma((2,)), dma((2,)),
            dma((4, 2)), dma((4, 2)), dma((4, 2)), dma((4, 2)),
            dma((8,)), dma((8,)),
            dma((7, 2)), dma((7, 2)),
            dma((n_exp // 2,)), dma((n_exp // 2,)), dma((n_exp,)), dma((n_exp,)),
            dma((2, 4, 2)), dma((2, 4, 2)), dma((RING, n_exp // 2)), dma((RING, n_exp // 2)),
        ],
        compiler_params=pltpu.CompilerParams(
            collective_id=0, has_side_effects=True, vmem_limit_bytes=60 * 2**20
        ),
    )(raw, far, w_in, w_down)


def per_device(tokens, out_grad, expert_ids, slots, gates, w_in, w_down):
    tok_count, width = tokens.shape
    half = width // 2
    top_count = expert_ids.shape[1]
    expert_count, blk_count = lax.axis_size("expert"), lax.axis_size("blk")
    capacity = max(2, (tok_count * top_count + expert_count - 1) // expert_count + 1)
    swap = [(i, (i + RING) % blk_count) for i in range(blk_count)]
    xl = lax.axis_index("blk") // RING

    share = width // THIRD

    def cut(x, dy, at, side):
        return [
            lax.dynamic_slice(x, (0, side * half), (tok_count, half)),
            lax.dynamic_slice(dy, (0, at + side * share), (tok_count, share)),
            dy[:, at + 2 * share : at + width],
        ]

    small = jnp.concatenate(
        [(expert_ids * (2 * capacity) + slots + capacity * xl).astype(jnp.bfloat16), gates], axis=1
    )
    small = jnp.pad(small, ((0, 0), (0, LANES - 2 * top_count)))
    away = jnp.concatenate([tokens, out_grad, small], axis=1)
    came = lax.ppermute(away, "blk", swap)
    small = jnp.concatenate([small, came[:, 2 * width :]], axis=0)
    target = small[:, :top_count].astype(jnp.int32)
    weight = small[:, top_count : 2 * top_count].astype(jnp.float32)
    slot_count = 2 * capacity
    n_tok = 2 * tok_count
    row = jnp.arange(expert_count * CHUNKS * slot_count, dtype=jnp.int32)
    row_target = row // (CHUNKS * slot_count) * slot_count + row % slot_count
    row_piece = row // slot_count % CHUNKS
    matches = (target[None] == row_target[:, None, None]).astype(jnp.float32)
    placing = jnp.sum(matches, axis=2)
    weighed = jnp.sum(matches * weight[None], axis=2)
    same = (row_piece[:, None] == jnp.arange(CHUNKS)[None]).astype(jnp.float32)

    def pieces(a):
        return (same[:, :, None] * a[:, None, :]).reshape(row.shape[0], CHUNKS * n_tok).astype(jnp.bfloat16)

    def stacked(side):
        rows = [cut(tokens, out_grad, 0, side), cut(came, came, width, side)]
        both = jnp.concatenate([jnp.concatenate(r, axis=1) for r in rows], axis=0)
        piece = both.shape[1] // CHUNKS
        return jnp.concatenate([both[:, k * piece : (k + 1) * piece] for k in range(CHUNKS)], axis=0)

    near = row.shape[0] // 2
    x_hi = lax.axis_index("expert") // (expert_count // 2)
    raw = stacked(xl)
    table = jnp.tile(small[:, :top_count].T, (1, CHUNKS))
    table = jnp.pad(table, ((0, 16 - top_count), (0, raw.shape[1] - table.shape[1])), constant_values=-1)
    raw = jnp.concatenate([raw, table], axis=0)
    far = lax.dynamic_slice(pieces(placing), ((1 - x_hi) * near, 0), (near, CHUNKS * n_tok))
    far = jnp.dot(far, stacked(1 - xl), preferred_element_type=jnp.float32).astype(jnp.bfloat16)
    back = expert_rows(raw, far, w_in[0], w_down[0], slot_count)
    part = half // CHUNKS
    grad = lax.dot_general(
        pieces(weighed), back[:, :part], (((0,), (0,)), ((), ())), preferred_element_type=jnp.float32
    ).astype(jnp.bfloat16)
    grad = jnp.concatenate([grad[k * n_tok : (k + 1) * n_tok] for k in range(CHUNKS)], axis=1)
    own, other = grad[:tok_count], grad[tok_count:]
    other = lax.ppermute(other, "blk", swap)
    grad_tokens = jnp.where(
        xl == 0, jnp.concatenate([own, other], axis=1), jnp.concatenate([other, own], axis=1)
    )
    first = (row_piece == 0).astype(jnp.float32) * back[:, part].astype(jnp.float32)
    grad_gates = jnp.einsum("stk,s->tk", matches[:, :tok_count], first).astype(jnp.bfloat16)
    return (grad_tokens, grad_gates)


def solution(mesh):
    return jax.shard_map(
        per_device,
        mesh=mesh,
        in_specs=(
            P(("expert", "blk"), None),
            P(("expert", "blk"), None),
            P(("expert", "blk"), None),
            P(("expert", "blk"), None),
            P(("expert", "blk"), None),
            P("expert", "blk", None),
            P("expert", "blk", None),
        ),
        out_specs=(P(("expert", "blk"), None), P(("expert", "blk"), None)),
        check_vma=False,
    )
```

```python
import functools

import jax
import jax.numpy as jnp
from jax import lax
from jax.experimental import pallas as pl
from jax.experimental.pallas import tpu as pltpu
from jax.sharding import PartitionSpec as P

MESH = pl.DeviceIdType.MESH
RING = 8
LANES = 128


def nt(a, b):
    return lax.dot_general(a, b, (((1,), (1,)), ((), ())), preferred_element_type=jnp.float32)


GROUPS = ((3, 0), (0, 0), (2, 0), (3, 1), (1, 0), (2, 1), (1, 1), (0, 1))
BEFORE = (None, None, (0, False), (1, True), (2, False), (3, False), (5, False))
CHUNKS = 8
THIRD = 3


def kernel(
    raw_ref, far_ref, win_ref, wdn_ref, out_ref,
    RAW, OUT, GOT, FAR, X, WI, WD, WP, PRE, BACK, ES, ER, SL, PART, SUM, ARR, MIX, TURN, TS,
    loc_sem, ws_sem, wr_sem, us_sem, ur_sem, ds_sem, dr_sem, es_sem, er_sem,
    ss_sem, sr_sem, as_sem, ar_sem, bs_sem, br_sem, ts_sem, tr_sem, ys_sem, yr_sem,
):
    half, hidden = WI.shape[2], WI.shape[1]
    R = X.shape[1] // 2
    U = R // 2
    bf16, f32 = jnp.bfloat16, jnp.float32
    n_exp = lax.axis_size("expert")
    me = lax.axis_index("expert")
    near = n_exp // 2
    side, seat = me // near, me % near
    blk = lax.axis_index("blk")
    xl, z = blk // RING, blk % RING
    above = {"blk": xl * RING + (z + 1) % RING}
    below = {"blk": xl * RING + (z + RING - 1) % RING}
    pair = {"blk": (1 - xl) * RING + z}

    def remote(src, dst, ss, rs, peer):
        return pltpu.make_async_remote_copy(
            src_ref=src, dst_ref=dst, send_sem=ss, recv_sem=rs, device_id=peer, device_id_type=MESH
        )

    def expert_loop(body):
        lax.fori_loop(1, n_exp, lambda j, c: (body(j), c)[1], 0)

    def greet(j):
        peer = {"expert": (me + j) % n_exp}
        pl.semaphore_signal(barrier, inc=1, device_id=peer, device_id_type=MESH)

    barrier = pltpu.get_barrier_semaphore()
    expert_loop(greet)
    for peer in (above, below, pair):
        pl.semaphore_signal(barrier, inc=1, device_id=peer, device_id_type=MESH)

    def across(j):
        return {"expert": (1 - side) * near + (seat + j) % near, "blk": (1 - xl) * RING + z}

    def greet_across(j, carry):
        pl.semaphore_signal(barrier, inc=1, device_id=across(j), device_id_type=MESH)
        return carry

    lax.fori_loop(0, near, greet_across, 0)

    T = far_ref.shape[0] // near

    def piece(e):
        return pl.ds(pl.multiple_of(e * T, 16), T)

    mine = pl.ds(pl.multiple_of(xl * half, LANES), half)
    theirs = pl.ds(pl.multiple_of((1 - xl) * half, LANES), half)
    own_raw = pltpu.make_async_copy(raw_ref, RAW.at[0], loc_sem.at[0])
    own_win = pltpu.make_async_copy(win_ref.at[:, mine], WI.at[xl], loc_sem.at[1])
    share = WP.shape[1]
    my_part = pl.ds(pl.multiple_of(xl * share, LANES), share)
    their_part = pl.ds(pl.multiple_of((1 - xl) * share, LANES), share)
    rest = pl.ds(2 * share, share)
    own_wdn = [
        pltpu.make_async_copy(wdn_ref.at[:, my_part], WD.at[:, pl.ds(0, share)], loc_sem.at[2]),
        pltpu.make_async_copy(wdn_ref.at[:, rest], WD.at[:, pl.ds(share, share)], loc_sem.at[4]),
    ]

    out_win = remote(win_ref.at[:, theirs], WI.at[xl], ws_sem.at[0], wr_sem.at[0], pair)
    out_wdn = remote(wdn_ref.at[:, their_part], WP, ws_sem.at[1], wr_sem.at[1], pair)
    in_win = remote(win_ref.at[:, mine], WI.at[1 - xl], ws_sem.at[0], wr_sem.at[0], pair)

    def to_far(j):
        e = (seat + j) % near
        return remote(far_ref.at[piece(e), :], FAR.at[piece(seat), :], as_sem.at[j], ar_sem.at[j], across(j))

    def to_near(r, j):
        e = (seat + j) % near
        return remote(
            OUT.at[r, piece(e), :], GOT.at[r, piece(seat), :], ys_sem.at[r, j], yr_sem.at[r, j],
            {"expert": side * near + e},
        )

    def near_own(r):
        return pltpu.make_async_copy(OUT.at[r, piece(seat), :], GOT.at[r, piece(seat), :], ys_sem.at[r, 0])

    def near_loop(r, body):
        lax.fori_loop(1, near, lambda j, c: (body(to_near(r, j)), c)[1], 0)

    def far_loop(body):
        lax.fori_loop(0, near, lambda j, c: (body(to_far(j)), c)[1], 0)

    def to_token(a, j):
        e = (seat + j) % near
        return remote(
            TS.at[piece(a * near + e), :], out_ref.at[piece(me), :], bs_sem.at[a, j], br_sem.at[a, j],
            {"expert": (side + a) % 2 * near + e},
        )

    def token_loop(a, body):
        lax.fori_loop(1 - a, near, lambda j, c: (body(to_token(a, j)), c)[1], 0)

    def raw_rows(a):
        return pl.ds(0, 80) if a == 0 else pl.ds(80, RAW.shape[1] - 80)

    def raw_up(s, a):
        return remote(
            RAW.at[s - 1, raw_rows(a), :], RAW.at[s, raw_rows(a), :], ts_sem.at[0, s - 1, a],
            tr_sem.at[0, s - 1, a], above,
        )

    def raw_down(s, a):
        src = 0 if s == 1 else RING // 2 + s - 1
        dst = RING // 2 + s if s < 4 else 4
        return remote(
            RAW.at[src, raw_rows(a), :], RAW.at[dst, raw_rows(a), :], ts_sem.at[1, s - 1, a],
            tr_sem.at[1, s - 1, a], below,
        )

    own_raw.start()
    own_raw.wait()
    pl.semaphore_wait(barrier, n_exp - 1 + 3 + near)
    raw_up(1, 0).start()
    raw_down(1, 1).start()
    raw_up(1, 1).start()
    raw_down(1, 0).start()
    far_loop(lambda c: c.start())
    out_win.start()
    own_win.start()
    for c in own_wdn:
        c.start()

    size = CHUNKS * U
    slots = T // CHUNKS
    row = lax.broadcasted_iota(jnp.int32, (size, 1), 0)
    partner = ((row // slots) % CHUNKS) * U + (row // U) * slots + row % slots
    MIX[...] = (lax.broadcasted_iota(jnp.int32, (size, size), 1) == partner).astype(f32).astype(bf16)

    tok = (RAW.shape[1] - 16) // CHUNKS
    wanted = ((side * near + row // T) * slots + row % slots).astype(f32)
    piece_of = (row // slots) % CHUNKS
    lane = lax.broadcasted_iota(jnp.int32, (1, CHUNKS * tok), 1) // tok

    def place(r):
        table = RAW[r, CHUNKS * tok : CHUNKS * tok + 16, : CHUNKS * tok].astype(f32)
        hit = jnp.zeros((size, CHUNKS * tok), f32)
        for k in range(4):
            hit = hit + (table[k : k + 1, :] == wanted).astype(f32)
        hit = jnp.where(piece_of == lane, hit, 0.0).astype(bf16)
        OUT[r] = jnp.dot(hit, RAW[r, : CHUNKS * tok, :], preferred_element_type=f32).astype(bf16)
        near_loop(r, lambda c: c.start())
        near_own(r).start()

    wide = FAR.shape[1]

    def turned(got, q, at):
        TURN[...] = jnp.dot(MIX[...], got, preferred_element_type=f32).astype(bf16)
        for k in range(CHUNKS):
            X[q, at : at + U, k * wide : (k + 1) * wide] = TURN[k * U : (k + 1) * U, :]

    def settle(r, q, at):
        near_own(r).wait()
        near_loop(r, lambda c: c.wait_recv())
        turned(GOT[r], q, at)

    def cols(a):
        return pl.ds(a * (X.shape[2] // 2), X.shape[2] // 2)

    def up(s, a):
        src = X.at[0, pl.ds(3 * U, U), cols(a)] if s == 1 else X.at[s - 1, pl.ds(2 * U, U), cols(a)]
        dst = X.at[s, pl.ds(2 * U, U), cols(a)] if s < 4 else X.at[0, pl.ds(U, U), cols(a)]
        return remote(src, dst, us_sem.at[s - 1, a], ur_sem.at[s - 1, a], above)

    def down(s, a):
        src = X.at[0, pl.ds(3 * U, U), cols(a)] if s == 1 else X.at[s - 1, pl.ds(U, U), cols(a)]
        dst = X.at[s % 4, pl.ds(U, U), cols(a)]
        return remote(src, dst, ds_sem.at[s - 1, a], dr_sem.at[s - 1, a], below)

    place(0)
    for s in range(1, 4):
        raw_up(s, 0).wait_recv()
        raw_up(s + 1, 0).start()
        raw_down(s, 1).wait_recv()
        raw_down(s + 1, 1).start()
        raw_up(s, 1).wait_recv()
        if s < 3:
            raw_up(s + 1, 1).start()
        raw_down(s, 0).wait_recv()
        if s < 3:
            raw_down(s + 1, 0).start()
        else:
            far_loop(lambda c: c.wait_recv())
            turned(FAR[...], 0, 3 * U)
            up(1, 0).start()
            down(1, 1).start()
            up(1, 1).start()
            down(1, 0).start()
        place(s)
        place(RING // 2 + s)
    raw_up(4, 0).wait_recv()
    raw_down(4, 1).wait_recv()
    place(4)
    own_win.wait()
    for c in own_wdn:
        c.wait()
    settle(0, 0, 2 * U)

    def project(q, at, n, h, what):
        rows = pl.ds(at, n)
        if "p" in what:
            PRE[q, h, rows, :] = nt(X[q, rows, :half], WI[h])
        if "b" in what:
            BACK[q, h, rows, :] = nt(X[q, rows, half:], WD[...])
        if "r" in what:
            BACK[q, h, rows, :] = nt(X[q, rows, half : half + share], WP[...])

    project(0, R, R, xl, "pb")
    for s in range(1, 4):
        up(s, 0).wait_recv()
        up(s + 1, 0).start()
        down(s, 1).wait_recv()
        down(s + 1, 1).start()
        up(s, 1).wait_recv()
        if s < 3:
            up(s + 1, 1).start()
        down(s, 0).wait_recv()
        if s < 3:
            down(s + 1, 0).start()
        if s == 1:
            out_wdn.start()
        settle(s, s, 0)
        settle(RING // 2 + s, s, 3 * U)
        project(s, 0, 2 * R, xl, "pb")
    in_win.wait_recv()
    for q in range(1, 4):
        project(q, 0, 2 * R, 1 - xl, "p")
    up(4, 0).wait_recv()
    down(4, 1).wait_recv()
    settle(4, 0, 0)
    project(0, 0, R, xl, "pb")
    project(0, 0, 2 * R, 1 - xl, "p")

    def swap(k):
        return remote(ES.at[k], ER.at[k], es_sem.at[k], er_sem.at[k], pair)

    def give(k):
        q, at = GROUPS[k][0], GROUPS[k][1] * R
        for h in range(2):
            ES[k, 0, h] = PRE[q, h, at : at + R, :].astype(bf16)
            ES[k, 1, h] = BACK[q, h, at : at + R, :].astype(bf16)
        swap(k).start()

    def terms(k):
        q, at = GROUPS[k][0], GROUPS[k][1] * R
        swap(k).wait_recv()
        if k + 2 < 8:
            give(k + 2)
        gate = jnp.zeros((R, 1), f32)
        for h in range(2):
            pre = PRE[q, h, at : at + R, :] + ER[k, 0, h].astype(f32)
            back = BACK[q, h, at : at + R, :] + ER[k, 1, h].astype(f32)
            sigma = jax.nn.sigmoid(pre)
            act = pre * sigma
            gate = gate + jnp.sum(act * back, axis=1, keepdims=True)
            SL[h] = (back * sigma * (1.0 + pre * (1.0 - sigma))).astype(bf16)
        PART[:, half:] = jnp.broadcast_to(gate, (R, LANES))
        step = 4 * LANES

        def columns(c, carry):
            there = pl.ds(pl.multiple_of(c * step, step), step)
            PART[:, there] = jnp.dot(SL[0], WI[0, :, there], preferred_element_type=f32) + jnp.dot(
                SL[1], WI[1, :, there], preferred_element_type=f32
            )
            return carry

        lax.fori_loop(0, half // step, columns, 0)

    def pass_on(k, a):
        rows = pl.ds(a * U, U)
        peer = above if (a == 0) == (k == 1) else below
        return remote(SUM.at[k, rows, :], ARR.at[k, rows, :], ss_sem.at[k, a], sr_sem.at[k, a], peer)

    def arrived(k, a):
        pass_on(k, a).wait_recv()
        return ARR[k, a * U : a * U + U, :].astype(f32)

    def add_and_pass(k):
        terms(k)
        for a in range(2):
            term = PART[a * U : a * U + U, :]
            if BEFORE[k] is not None:
                b, crossed = BEFORE[k]
                term = term + arrived(b, 1 - a if crossed else a)
            SUM[k, a * U : a * U + U, :] = term.astype(bf16)
            pass_on(k, a).start()

    out_wdn.wait_recv()
    project(3, 0, 2 * R, 1 - xl, "r")
    give(0)
    project(0, 0, 2 * R, 1 - xl, "r")
    give(1)
    project(2, 0, 2 * R, 1 - xl, "r")
    project(1, 0, 2 * R, 1 - xl, "r")
    for k in range(7):
        add_and_pass(k)
    terms(7)

    for a in range(2):
        total = (PART[a * U : a * U + U, :] + arrived(4, a) + arrived(6, 1 - a)).astype(bf16)
        third = half // CHUNKS
        for k in range(CHUNKS):
            TURN[k * U : (k + 1) * U, :third] = total[:, k * third : (k + 1) * third]
            TURN[k * U : (k + 1) * U, third : third + LANES] = total[:, half:]
        TS[a * size : a * size + size, :] = jnp.dot(
            MIX[...], TURN[:, : third + LANES], preferred_element_type=f32
        ).astype(bf16)
        token_loop(a, lambda c: c.start())
    own_back = pltpu.make_async_copy(TS.at[piece(seat), :], out_ref.at[piece(me), :], loc_sem.at[3])
    own_back.start()

    out_win.wait_send()
    out_wdn.wait_send()
    far_loop(lambda c: c.wait_send())
    for r in range(RING):
        near_loop(r, lambda c: c.wait_send())
    for s in range(1, 5):
        for a in range(2):
            if s < 4 or a == 0:
                raw_up(s, a).wait_send()
            if s < 4 or a == 1:
                raw_down(s, a).wait_send()
    for s in range(1, 5):
        for u in range(2):
            if s < 4 or u == 0:
                up(s, u).wait_send()
            if s < 4 or u == 1:
                down(s, u).wait_send()
    for k in range(8):
        swap(k).wait_send()
    for k in range(7):
        for a in range(2):
            pass_on(k, a).wait_send()
    own_back.wait()
    for a in range(2):
        token_loop(a, lambda c: c.wait())


def expert_rows(raw, far, w_in, w_down, slots):
    n_exp = lax.axis_size("expert")
    hidden, width = w_in.shape
    half = width // 2
    n_rows = n_exp * slots
    wide = half + LANES
    back = half // CHUNKS + LANES
    bf16, f32, dma = jnp.bfloat16, jnp.float32, pltpu.SemaphoreType.DMA
    return pl.pallas_call(
        kernel,
        out_shape=jax.ShapeDtypeStruct((2 * far.shape[0], back), bf16),
        in_specs=[pl.BlockSpec(memory_space=pl.ANY)] * 4,
        out_specs=pl.BlockSpec(memory_space=pltpu.VMEM),
        scratch_shapes=[
            pltpu.VMEM((RING,) + raw.shape, bf16),
            pltpu.VMEM((RING,) + far.shape, bf16),
            pltpu.VMEM((RING,) + far.shape, bf16),
            pltpu.VMEM(far.shape, bf16),
            pltpu.VMEM((4, 2 * n_rows, CHUNKS * raw.shape[1]), bf16),
            pltpu.VMEM((2, hidden, half), bf16),
            pltpu.VMEM((hidden, 2 * width // THIRD), bf16),
            pltpu.VMEM((hidden, width // THIRD), bf16),
            pltpu.VMEM((4, 2, 2 * n_rows, hidden), f32),
            pltpu.VMEM((4, 2, 2 * n_rows, hidden), f32),
            pltpu.VMEM((8, 2, 2, n_rows, hidden), bf16),
            pltpu.VMEM((8, 2, 2, n_rows, hidden), bf16),
            pltpu.VMEM((2, n_rows, hidden), bf16),
            pltpu.VMEM((n_rows, wide), f32),
            pltpu.VMEM((7, n_rows, wide), bf16),
            pltpu.VMEM((7, n_rows, wide), bf16),
            pltpu.VMEM((far.shape[0], far.shape[0]), bf16),
            pltpu.VMEM(far.shape, bf16),
            pltpu.VMEM((2 * far.shape[0], back), bf16),
            dma((5,)), dma((2,)), dma((2,)),
            dma((4, 2)), dma((4, 2)), dma((4, 2)), dma((4, 2)),
            dma((8,)), dma((8,)),
            dma((7, 2)), dma((7, 2)),
            dma((n_exp // 2,)), dma((n_exp // 2,)), dma((2, n_exp // 2)), dma((2, n_exp // 2)),
            dma((2, 4, 2)), dma((2, 4, 2)), dma((RING, n_exp // 2)), dma((RING, n_exp // 2)),
        ],
        compiler_params=pltpu.CompilerParams(
            collective_id=0, has_side_effects=True, vmem_limit_bytes=60 * 2**20
        ),
    )(raw, far, w_in, w_down)


def per_device(tokens, out_grad, expert_ids, slots, gates, w_in, w_down):
    tok_count, width = tokens.shape
    half = width // 2
    top_count = expert_ids.shape[1]
    expert_count, blk_count = lax.axis_size("expert"), lax.axis_size("blk")
    capacity = max(2, (tok_count * top_count + expert_count - 1) // expert_count + 1)
    swap = [(i, (i + RING) % blk_count) for i in range(blk_count)]
    xl = lax.axis_index("blk") // RING

    share = width // THIRD

    def cut(x, dy, side):
        return [
            lax.dynamic_slice(x, (0, side * half), (tok_count, half)),
            lax.dynamic_slice(dy, (0, side * share), (tok_count, share)),
            dy[:, 2 * share :],
        ]

    small = jnp.concatenate(
        [(expert_ids * (2 * capacity) + slots + capacity * xl).T.astype(jnp.bfloat16), gates.T], axis=0
    )
    came = [lax.ppermute(a, "blk", swap) for a in (small, tokens, out_grad)]
    small = jnp.concatenate([small, came[0]], axis=1)
    target = small[:top_count].astype(jnp.int32)
    weight = small[top_count:].astype(jnp.float32)
    slot_count = 2 * capacity
    n_tok = 2 * tok_count
    row = jnp.arange(expert_count * CHUNKS * slot_count, dtype=jnp.int32)
    row_target = row // (CHUNKS * slot_count) * slot_count + row % slot_count
    row_piece = row // slot_count % CHUNKS
    matches = (target[None] == row_target[:, None, None]).astype(jnp.float32)
    placing = jnp.sum(matches, axis=1)
    weighed = jnp.sum(matches * weight[None], axis=1)
    same = (row_piece[:, None] == jnp.arange(CHUNKS)[None]).astype(jnp.float32)

    def pieces(a):
        return (same[:, :, None] * a[:, None, :]).reshape(row.shape[0], CHUNKS * n_tok).astype(jnp.bfloat16)

    def stacked(side):
        rows = [cut(tokens, out_grad, side), cut(came[1], came[2], side)]
        both = jnp.concatenate([jnp.concatenate(r, axis=1) for r in rows], axis=0)
        piece = both.shape[1] // CHUNKS
        return jnp.concatenate([both[:, k * piece : (k + 1) * piece] for k in range(CHUNKS)], axis=0)

    near = row.shape[0] // 2
    x_hi = lax.axis_index("expert") // (expert_count // 2)
    raw = stacked(xl)
    table = jnp.tile(small[:top_count], (1, CHUNKS))
    table = jnp.pad(table, ((0, 16 - top_count), (0, raw.shape[1] - table.shape[1])), constant_values=-1)
    raw = jnp.concatenate([raw, table], axis=0)
    far = lax.dynamic_slice(pieces(placing), ((1 - x_hi) * near, 0), (near, CHUNKS * n_tok))
    far = jnp.dot(far, stacked(1 - xl), preferred_element_type=jnp.float32).astype(jnp.bfloat16)
    back = expert_rows(raw, far, w_in[0], w_down[0], slot_count)
    part = half // CHUNKS
    grad = lax.dot_general(
        pieces(weighed), back[:, :part], (((0,), (0,)), ((), ())), preferred_element_type=jnp.float32
    ).astype(jnp.bfloat16)
    grad = jnp.concatenate([grad[k * n_tok : (k + 1) * n_tok] for k in range(CHUNKS)], axis=1)
    own, other = grad[:tok_count], grad[tok_count:]
    other = lax.ppermute(other, "blk", swap)
    grad_tokens = jnp.where(
        xl == 0, jnp.concatenate([own, other], axis=1), jnp.concatenate([other, own], axis=1)
    )
    first = (row_piece == 0).astype(jnp.float32) * back[:, part].astype(jnp.float32)
    grad_gates = jnp.einsum("skt,s->tk", matches[:, :, :tok_count], first).astype(jnp.bfloat16)
    return (grad_tokens, grad_gates)


def solution(mesh):
    return jax.shard_map(
        per_device,
        mesh=mesh,
        in_specs=(
            P(("expert", "blk"), None),
            P(("expert", "blk"), None),
            P(("expert", "blk"), None),
            P(("expert", "blk"), None),
            P(("expert", "blk"), None),
            P("expert", "blk", None),
            P("expert", "blk", None),
        ),
        out_specs=(P(("expert", "blk"), None), P(("expert", "blk"), None)),
        check_vma=False,
    )
```

```python
import functools

import jax
import jax.numpy as jnp
from jax import lax
from jax.experimental import pallas as pl
from jax.experimental.pallas import tpu as pltpu
from jax.sharding import PartitionSpec as P

MESH = pl.DeviceIdType.MESH
RING = 8
LANES = 128


def nt(a, b):
    return lax.dot_general(a, b, (((1,), (1,)), ((), ())), preferred_element_type=jnp.float32)


GROUPS = ((3, 0), (0, 0), (2, 0), (3, 1), (1, 0), (2, 1), (1, 1), (0, 1))
BEFORE = (None, None, (0, False), (1, True), (2, False), (3, False), (5, False))
CHUNKS = 8
THIRD = 3


def kernel(
    raw_ref, far_ref, win_ref, wdn_ref, out_ref,
    RAW, OUT, GOT, FAR, X, WI, WD, WP, PRE, BACK, ES, ER, SL, PART, SUM, ARR, MIX, TURN, TS,
    loc_sem, ws_sem, wr_sem, us_sem, ur_sem, ds_sem, dr_sem, es_sem, er_sem,
    ss_sem, sr_sem, as_sem, ar_sem, bs_sem, br_sem, ts_sem, tr_sem, ys_sem, yr_sem,
):
    half, hidden = WI.shape[2], WI.shape[1]
    R = X.shape[1] // 2
    U = R // 2
    bf16, f32 = jnp.bfloat16, jnp.float32
    n_exp = lax.axis_size("expert")
    me = lax.axis_index("expert")
    near = n_exp // 2
    side, seat = me // near, me % near
    blk = lax.axis_index("blk")
    xl, z = blk // RING, blk % RING
    above = {"blk": xl * RING + (z + 1) % RING}
    below = {"blk": xl * RING + (z + RING - 1) % RING}
    pair = {"blk": (1 - xl) * RING + z}

    def remote(src, dst, ss, rs, peer):
        return pltpu.make_async_remote_copy(
            src_ref=src, dst_ref=dst, send_sem=ss, recv_sem=rs, device_id=peer, device_id_type=MESH
        )

    def expert_loop(body):
        lax.fori_loop(1, n_exp, lambda j, c: (body(j), c)[1], 0)

    def greet(j):
        peer = {"expert": (me + j) % n_exp}
        pl.semaphore_signal(barrier, inc=1, device_id=peer, device_id_type=MESH)

    barrier = pltpu.get_barrier_semaphore()
    expert_loop(greet)
    for peer in (above, below, pair):
        pl.semaphore_signal(barrier, inc=1, device_id=peer, device_id_type=MESH)

    def across(j):
        return {"expert": (1 - side) * near + (seat + j) % near, "blk": (1 - xl) * RING + z}

    def greet_across(j, carry):
        pl.semaphore_signal(barrier, inc=1, device_id=across(j), device_id_type=MESH)
        return carry

    lax.fori_loop(0, near, greet_across, 0)

    T = far_ref.shape[0] // near

    def piece(e):
        return pl.ds(pl.multiple_of(e * T, 16), T)

    mine = pl.ds(pl.multiple_of(xl * half, LANES), half)
    theirs = pl.ds(pl.multiple_of((1 - xl) * half, LANES), half)
    own_raw = pltpu.make_async_copy(raw_ref, RAW.at[0], loc_sem.at[0])
    own_win = pltpu.make_async_copy(win_ref.at[:, mine], WI.at[xl], loc_sem.at[1])
    share = WP.shape[1]
    my_part = pl.ds(pl.multiple_of(xl * share, LANES), share)
    their_part = pl.ds(pl.multiple_of((1 - xl) * share, LANES), share)
    rest = pl.ds(2 * share, share)
    own_wdn = [
        pltpu.make_async_copy(wdn_ref.at[:, my_part], WD.at[:, pl.ds(0, share)], loc_sem.at[2]),
        pltpu.make_async_copy(wdn_ref.at[:, rest], WD.at[:, pl.ds(share, share)], loc_sem.at[4]),
    ]

    out_win = remote(win_ref.at[:, theirs], WI.at[xl], ws_sem.at[0], wr_sem.at[0], pair)
    out_wdn = remote(wdn_ref.at[:, their_part], WP, ws_sem.at[1], wr_sem.at[1], pair)
    in_win = remote(win_ref.at[:, mine], WI.at[1 - xl], ws_sem.at[0], wr_sem.at[0], pair)

    def to_far(j):
        e = (seat + j) % near
        return remote(far_ref.at[piece(e), :], FAR.at[piece(seat), :], as_sem.at[j], ar_sem.at[j], across(j))

    def to_near(r, j):
        e = (seat + j) % near
        return remote(
            OUT.at[r, piece(e), :], GOT.at[r, piece(seat), :], ys_sem.at[r, j], yr_sem.at[r, j],
            {"expert": side * near + e},
        )

    def near_own(r):
        return pltpu.make_async_copy(OUT.at[r, piece(seat), :], GOT.at[r, piece(seat), :], ys_sem.at[r, 0])

    def near_loop(r, body):
        lax.fori_loop(1, near, lambda j, c: (body(to_near(r, j)), c)[1], 0)

    def far_loop(body):
        lax.fori_loop(0, near, lambda j, c: (body(to_far(j)), c)[1], 0)

    def to_token(a, j):
        e = (seat + j) % near
        return remote(
            TS.at[piece(a * near + e), :], out_ref.at[piece(me), :], bs_sem.at[a, j], br_sem.at[a, j],
            {"expert": (side + a) % 2 * near + e},
        )

    def token_loop(a, body):
        lax.fori_loop(1 - a, near, lambda j, c: (body(to_token(a, j)), c)[1], 0)

    def raw_rows(a):
        return pl.ds(0, 80) if a == 0 else pl.ds(80, RAW.shape[1] - 80)

    def raw_up(s, a):
        return remote(
            RAW.at[s - 1, raw_rows(a), :], RAW.at[s, raw_rows(a), :], ts_sem.at[0, s - 1, a],
            tr_sem.at[0, s - 1, a], above,
        )

    def raw_down(s, a):
        src = 0 if s == 1 else RING // 2 + s - 1
        dst = RING // 2 + s if s < 4 else 4
        return remote(
            RAW.at[src, raw_rows(a), :], RAW.at[dst, raw_rows(a), :], ts_sem.at[1, s - 1, a],
            tr_sem.at[1, s - 1, a], below,
        )

    own_raw.start()
    own_raw.wait()
    pl.semaphore_wait(barrier, n_exp - 1 + 3 + near)
    raw_up(1, 0).start()
    raw_down(1, 1).start()
    raw_up(1, 1).start()
    raw_down(1, 0).start()
    far_loop(lambda c: c.start())
    out_win.start()
    out_wdn.start()
    own_win.start()
    for c in own_wdn:
        c.start()

    size = CHUNKS * U
    slots = T // CHUNKS
    row = lax.broadcasted_iota(jnp.int32, (size, 1), 0)
    partner = ((row // slots) % CHUNKS) * U + (row // U) * slots + row % slots
    MIX[...] = (lax.broadcasted_iota(jnp.int32, (size, size), 1) == partner).astype(f32).astype(bf16)

    tok = (RAW.shape[1] - 16) // CHUNKS
    wanted = ((side * near + row // T) * slots + row % slots).astype(f32)
    piece_of = (row // slots) % CHUNKS
    lane = lax.broadcasted_iota(jnp.int32, (1, CHUNKS * tok), 1) // tok

    def place(r):
        table = RAW[r, CHUNKS * tok : CHUNKS * tok + 16, : CHUNKS * tok].astype(f32)
        hit = jnp.zeros((size, CHUNKS * tok), f32)
        for k in range(4):
            hit = hit + (table[k : k + 1, :] == wanted).astype(f32)
        hit = jnp.where(piece_of == lane, hit, 0.0).astype(bf16)
        OUT[r] = jnp.dot(hit, RAW[r, : CHUNKS * tok, :], preferred_element_type=f32).astype(bf16)
        near_loop(r, lambda c: c.start())
        near_own(r).start()

    wide = FAR.shape[1]

    def turned(got, q, at):
        TURN[...] = jnp.dot(MIX[...], got, preferred_element_type=f32).astype(bf16)
        for k in range(CHUNKS):
            X[q, at : at + U, k * wide : (k + 1) * wide] = TURN[k * U : (k + 1) * U, :]

    def settle(r, q, at):
        near_own(r).wait()
        near_loop(r, lambda c: c.wait_recv())
        turned(GOT[r], q, at)

    def cols(a):
        return pl.ds(a * (X.shape[2] // 2), X.shape[2] // 2)

    def up(s, a):
        src = X.at[0, pl.ds(3 * U, U), cols(a)] if s == 1 else X.at[s - 1, pl.ds(2 * U, U), cols(a)]
        dst = X.at[s, pl.ds(2 * U, U), cols(a)] if s < 4 else X.at[0, pl.ds(U, U), cols(a)]
        return remote(src, dst, us_sem.at[s - 1, a], ur_sem.at[s - 1, a], above)

    def down(s, a):
        src = X.at[0, pl.ds(3 * U, U), cols(a)] if s == 1 else X.at[s - 1, pl.ds(U, U), cols(a)]
        dst = X.at[s % 4, pl.ds(U, U), cols(a)]
        return remote(src, dst, ds_sem.at[s - 1, a], dr_sem.at[s - 1, a], below)

    place(0)
    for s in range(1, 4):
        raw_up(s, 0).wait_recv()
        raw_up(s + 1, 0).start()
        raw_down(s, 1).wait_recv()
        raw_down(s + 1, 1).start()
        raw_up(s, 1).wait_recv()
        if s < 3:
            raw_up(s + 1, 1).start()
        raw_down(s, 0).wait_recv()
        if s < 3:
            raw_down(s + 1, 0).start()
        else:
            far_loop(lambda c: c.wait_recv())
            turned(FAR[...], 0, 3 * U)
            up(1, 0).start()
            down(1, 1).start()
            up(1, 1).start()
            down(1, 0).start()
        place(s)
        place(RING // 2 + s)
    raw_up(4, 0).wait_recv()
    raw_down(4, 1).wait_recv()
    place(4)
    own_win.wait()
    for c in own_wdn:
        c.wait()
    settle(0, 0, 2 * U)

    def project(q, at, n, h, what):
        rows = pl.ds(at, n)
        if "p" in what:
            PRE[q, h, rows, :] = nt(X[q, rows, :half], WI[h])
        if "b" in what:
            BACK[q, h, rows, :] = nt(X[q, rows, half:], WD[...])
        if "r" in what:
            BACK[q, h, rows, :] = nt(X[q, rows, half : half + share], WP[...])

    project(0, R, R, xl, "pb")
    for s in range(1, 4):
        up(s, 0).wait_recv()
        up(s + 1, 0).start()
        down(s, 1).wait_recv()
        down(s + 1, 1).start()
        up(s, 1).wait_recv()
        if s < 3:
            up(s + 1, 1).start()
        down(s, 0).wait_recv()
        if s < 3:
            down(s + 1, 0).start()
        settle(s, s, 0)
        settle(RING // 2 + s, s, 3 * U)
        project(s, 0, 2 * R, xl, "pb")
    in_win.wait_recv()
    for q in range(1, 4):
        project(q, 0, 2 * R, 1 - xl, "p")
    up(4, 0).wait_recv()
    down(4, 1).wait_recv()
    settle(4, 0, 0)
    project(0, 0, R, xl, "pb")
    project(0, 0, 2 * R, 1 - xl, "p")

    def swap(k):
        return remote(ES.at[k], ER.at[k], es_sem.at[k], er_sem.at[k], pair)

    def give(k):
        q, at = GROUPS[k][0], GROUPS[k][1] * R
        for h in range(2):
            ES[k, 0, h] = PRE[q, h, at : at + R, :].astype(bf16)
            ES[k, 1, h] = BACK[q, h, at : at + R, :].astype(bf16)
        swap(k).start()

    def terms(k):
        q, at = GROUPS[k][0], GROUPS[k][1] * R
        swap(k).wait_recv()
        if k + 2 < 8:
            give(k + 2)
        gate = jnp.zeros((R, 1), f32)
        for h in range(2):
            pre = PRE[q, h, at : at + R, :] + ER[k, 0, h].astype(f32)
            back = BACK[q, h, at : at + R, :] + ER[k, 1, h].astype(f32)
            sigma = jax.nn.sigmoid(pre)
            act = pre * sigma
            gate = gate + jnp.sum(act * back, axis=1, keepdims=True)
            SL[h] = (back * sigma * (1.0 + pre * (1.0 - sigma))).astype(bf16)
        PART[:, half:] = jnp.broadcast_to(gate, (R, LANES))
        step = 4 * LANES

        def columns(c, carry):
            there = pl.ds(pl.multiple_of(c * step, step), step)
            PART[:, there] = jnp.dot(SL[0], WI[0, :, there], preferred_element_type=f32) + jnp.dot(
                SL[1], WI[1, :, there], preferred_element_type=f32
            )
            return carry

        lax.fori_loop(0, half // step, columns, 0)

    def pass_on(k, a):
        rows = pl.ds(a * U, U)
        peer = above if (a == 0) == (k == 1) else below
        return remote(SUM.at[k, rows, :], ARR.at[k, rows, :], ss_sem.at[k, a], sr_sem.at[k, a], peer)

    def arrived(k, a):
        pass_on(k, a).wait_recv()
        return ARR[k, a * U : a * U + U, :].astype(f32)

    def add_and_pass(k):
        terms(k)
        for a in range(2):
            term = PART[a * U : a * U + U, :]
            if BEFORE[k] is not None:
                b, crossed = BEFORE[k]
                term = term + arrived(b, 1 - a if crossed else a)
            SUM[k, a * U : a * U + U, :] = term.astype(bf16)
            pass_on(k, a).start()

    out_wdn.wait_recv()
    project(3, 0, 2 * R, 1 - xl, "r")
    give(0)
    project(0, 0, 2 * R, 1 - xl, "r")
    give(1)
    project(2, 0, 2 * R, 1 - xl, "r")
    project(1, 0, 2 * R, 1 - xl, "r")
    for k in range(7):
        add_and_pass(k)
    terms(7)

    for a in range(2):
        total = (PART[a * U : a * U + U, :] + arrived(4, a) + arrived(6, 1 - a)).astype(bf16)
        third = half // CHUNKS
        for k in range(CHUNKS):
            TURN[k * U : (k + 1) * U, :third] = total[:, k * third : (k + 1) * third]
            TURN[k * U : (k + 1) * U, third : third + LANES] = total[:, half:]
        TS[a * size : a * size + size, :] = jnp.dot(
            MIX[...], TURN[:, : third + LANES], preferred_element_type=f32
        ).astype(bf16)
        token_loop(a, lambda c: c.start())
    own_back = pltpu.make_async_copy(TS.at[piece(seat), :], out_ref.at[piece(me), :], loc_sem.at[3])
    own_back.start()

    out_win.wait_send()
    out_wdn.wait_send()
    far_loop(lambda c: c.wait_send())
    for r in range(RING):
        near_loop(r, lambda c: c.wait_send())
    for s in range(1, 5):
        for a in range(2):
            if s < 4 or a == 0:
                raw_up(s, a).wait_send()
            if s < 4 or a == 1:
                raw_down(s, a).wait_send()
    for s in range(1, 5):
        for u in range(2):
            if s < 4 or u == 0:
                up(s, u).wait_send()
            if s < 4 or u == 1:
                down(s, u).wait_send()
    for k in range(8):
        swap(k).wait_send()
    for k in range(7):
        for a in range(2):
            pass_on(k, a).wait_send()
    own_back.wait()
    for a in range(2):
        token_loop(a, lambda c: c.wait())


def expert_rows(raw, far, w_in, w_down, slots):
    n_exp = lax.axis_size("expert")
    hidden, width = w_in.shape
    half = width // 2
    n_rows = n_exp * slots
    wide = half + LANES
    back = half // CHUNKS + LANES
    bf16, f32, dma = jnp.bfloat16, jnp.float32, pltpu.SemaphoreType.DMA
    return pl.pallas_call(
        kernel,
        out_shape=jax.ShapeDtypeStruct((2 * far.shape[0], back), bf16),
        in_specs=[pl.BlockSpec(memory_space=pl.ANY)] * 4,
        out_specs=pl.BlockSpec(memory_space=pltpu.VMEM),
        scratch_shapes=[
            pltpu.VMEM((RING,) + raw.shape, bf16),
            pltpu.VMEM((RING,) + far.shape, bf16),
            pltpu.VMEM((RING,) + far.shape, bf16),
            pltpu.VMEM(far.shape, bf16),
            pltpu.VMEM((4, 2 * n_rows, CHUNKS * raw.shape[1]), bf16),
            pltpu.VMEM((2, hidden, half), bf16),
            pltpu.VMEM((hidden, 2 * width // THIRD), bf16),
            pltpu.VMEM((hidden, width // THIRD), bf16),
            pltpu.VMEM((4, 2, 2 * n_rows, hidden), f32),
            pltpu.VMEM((4, 2, 2 * n_rows, hidden), f32),
            pltpu.VMEM((8, 2, 2, n_rows, hidden), bf16),
            pltpu.VMEM((8, 2, 2, n_rows, hidden), bf16),
            pltpu.VMEM((2, n_rows, hidden), bf16),
            pltpu.VMEM((n_rows, wide), f32),
            pltpu.VMEM((7, n_rows, wide), bf16),
            pltpu.VMEM((7, n_rows, wide), bf16),
            pltpu.VMEM((far.shape[0], far.shape[0]), bf16),
            pltpu.VMEM(far.shape, bf16),
            pltpu.VMEM((2 * far.shape[0], back), bf16),
            dma((5,)), dma((2,)), dma((2,)),
            dma((4, 2)), dma((4, 2)), dma((4, 2)), dma((4, 2)),
            dma((8,)), dma((8,)),
            dma((7, 2)), dma((7, 2)),
            dma((n_exp // 2,)), dma((n_exp // 2,)), dma((2, n_exp // 2)), dma((2, n_exp // 2)),
            dma((2, 4, 2)), dma((2, 4, 2)), dma((RING, n_exp // 2)), dma((RING, n_exp // 2)),
        ],
        compiler_params=pltpu.CompilerParams(
            collective_id=0, has_side_effects=True, vmem_limit_bytes=60 * 2**20
        ),
    )(raw, far, w_in, w_down)


def per_device(tokens, out_grad, expert_ids, slots, gates, w_in, w_down):
    tok_count, width = tokens.shape
    half = width // 2
    top_count = expert_ids.shape[1]
    expert_count, blk_count = lax.axis_size("expert"), lax.axis_size("blk")
    capacity = max(2, (tok_count * top_count + expert_count - 1) // expert_count + 1)
    swap = [(i, (i + RING) % blk_count) for i in range(blk_count)]
    xl = lax.axis_index("blk") // RING

    share = width // THIRD

    def cut(x, dy, side):
        return [
            lax.dynamic_slice(x, (0, side * half), (tok_count, half)),
            lax.dynamic_slice(dy, (0, side * share), (tok_count, share)),
            dy[:, 2 * share :],
        ]

    small = jnp.concatenate(
        [(expert_ids * (2 * capacity) + slots + capacity * xl).T.astype(jnp.bfloat16), gates.T], axis=0
    )
    came = [lax.ppermute(a, "blk", swap) for a in (small, tokens, out_grad)]
    small = jnp.concatenate([small, came[0]], axis=1)
    target = small[:top_count].astype(jnp.int32)
    weight = small[top_count:].astype(jnp.float32)
    slot_count = 2 * capacity
    n_tok = 2 * tok_count
    row = jnp.arange(expert_count * CHUNKS * slot_count, dtype=jnp.int32)
    row_target = row // (CHUNKS * slot_count) * slot_count + row % slot_count
    row_piece = row // slot_count % CHUNKS
    matches = (target[None] == row_target[:, None, None]).astype(jnp.float32)
    placing = jnp.sum(matches, axis=1)
    weighed = jnp.sum(matches * weight[None], axis=1)
    same = (row_piece[:, None] == jnp.arange(CHUNKS)[None]).astype(jnp.float32)

    def pieces(a):
        return (same[:, :, None] * a[:, None, :]).reshape(row.shape[0], CHUNKS * n_tok).astype(jnp.bfloat16)

    def stacked(side):
        rows = [cut(tokens, out_grad, side), cut(came[1], came[2], side)]
        both = jnp.concatenate([jnp.concatenate(r, axis=1) for r in rows], axis=0)
        piece = both.shape[1] // CHUNKS
        return jnp.concatenate([both[:, k * piece : (k + 1) * piece] for k in range(CHUNKS)], axis=0)

    near = row.shape[0] // 2
    x_hi = lax.axis_index("expert") // (expert_count // 2)
    raw = stacked(xl)
    table = jnp.tile(small[:top_count], (1, CHUNKS))
    table = jnp.pad(table, ((0, 16 - top_count), (0, raw.shape[1] - table.shape[1])), constant_values=-1)
    raw = jnp.concatenate([raw, table], axis=0)
    far = lax.dynamic_slice(pieces(placing), ((1 - x_hi) * near, 0), (near, CHUNKS * n_tok))
    far = jnp.dot(far, stacked(1 - xl), preferred_element_type=jnp.float32).astype(jnp.bfloat16)
    back = expert_rows(raw, far, w_in[0], w_down[0], slot_count)
    part = half // CHUNKS
    grad = lax.dot_general(
        pieces(weighed), back[:, :part], (((0,), (0,)), ((), ())), preferred_element_type=jnp.float32
    ).astype(jnp.bfloat16)
    grad = jnp.concatenate([grad[k * n_tok : (k + 1) * n_tok] for k in range(CHUNKS)], axis=1)
    own, other = grad[:tok_count], grad[tok_count:]
    other = lax.ppermute(other, "blk", swap)
    grad_tokens = jnp.where(
        xl == 0, jnp.concatenate([own, other], axis=1), jnp.concatenate([other, own], axis=1)
    )
    first = (row_piece == 0).astype(jnp.float32) * back[:, part].astype(jnp.float32)
    grad_gates = jnp.einsum("skt,s->tk", matches[:, :, :tok_count], first).astype(jnp.bfloat16)
    return (grad_tokens, grad_gates)


def solution(mesh):
    return jax.shard_map(
        per_device,
        mesh=mesh,
        in_specs=(
            P(("expert", "blk"), None),
            P(("expert", "blk"), None),
            P(("expert", "blk"), None),
            P(("expert", "blk"), None),
            P(("expert", "blk"), None),
            P("expert", "blk", None),
            P("expert", "blk", None),
        ),
        out_specs=(P(("expert", "blk"), None), P(("expert", "blk"), None)),
        check_vma=False,
    )
```
